128 devices in a mesh: wide: 8 (over z, core), narrow: 16 (over y, x).
Axes of the slice: x: 4, y: 4, z: 4, core: 2. Of those that a mesh axis runs over, the one named last changes fastest.
Arguments:
- source: float32 [128, 512, 128], P('wide', 'narrow'), may hold values from -8 to 8
- conduct: float32 [128, 512, 128], P('wide', 'narrow'), may hold values from 0.5 to 2
- storage: float32 [128, 512, 128], P('wide', 'narrow'), may hold values from 0.25 to 2
Outputs:
- correction: float32 [128, 512, 128], P('wide', 'narrow')
- remainder: float32 [128, 512, 128], P('wide', 'narrow')
- upper: float32 [9, 9], replicated
- residual_norm: float32 [], replicated
The draws below stay inside these ranges and needn't reach their ends.
All inputs are finite; a program needn't handle non-finite values.
Results may differ from the reference program's by a relative error of at most 0.039.
Values sent between devices are 32-bit elements; how exact they have to be, the bound alone decides.
No kernel may reach another device: no remote copies, remote signals or barrier semaphores. Data moves between devices by JAX's collectives and lax.ppermute only.
A program may use at most 128 MiB of HBM per device.

```python
import math
import jax
import jax.numpy as jnp
import numpy as np
from jax import lax

STEPS = 8
COLS = 9
NX = 128
NY = 512
NZ = 128


def plane_weights(count):
    table = np.array([0.05, 1.0, 0.05, 0.05, 0.05, 1.0, 0.05, 1.0, 0.05, 0.05, 0.05, 1.0], dtype=np.float32)
    return jnp.asarray(table)[jnp.arange(count) % 12]


def draw_source(key, part):
    key = jax.random.fold_in(key, 11)
    values = jnp.clip(jax.random.normal(key, (NX, NY, NZ), jnp.float32), -8.0, 8.0)
    scale = plane_weights(NZ)
    return (values * scale[None, None, :]).astype(jnp.float32)


def shard_levels(rng, dims, split, low, high):
    factor_of = 1.0
    for axis_at, blocks in split:
        heights = jax.random.uniform(jax.random.fold_in(jax.random.fold_in(rng, 6), axis_at), (blocks,), jnp.float32, low / len(split), high / len(split))
        factor_of = factor_of * jnp.repeat(jnp.exp(heights), dims[axis_at] // blocks).reshape((-1,) + (1,) * (len(dims) - 1 - axis_at))
    return factor_of


def setup_inputs(seed: int = 0) -> dict:
    streams_of = jax.random.split(jax.random.key(seed), 4)
    source = draw_source(jax.random.fold_in(streams_of[3], 71), 0)
    conduct = jnp.clip(jnp.exp(math.log(2.0) - 1.3862944 * jax.random.uniform(streams_of[1], (NX, NY, NZ), jnp.float32) ** shard_levels(streams_of[1], (NX, NY, NZ), ((0, 8), (1, 16)), -0.2, 0.2)), 0.5, 2.0)
    storage = jnp.clip(jnp.exp(math.log(2.0) - 2.0794415 * jax.random.uniform(streams_of[2], (NX, NY, NZ), jnp.float32) ** shard_levels(streams_of[2], (NX, NY, NZ), ((0, 8), (1, 16)), -0.2, 0.2)), 0.25, 2.0)
    return dict(source=source, conduct=conduct, storage=storage)


HIGH = lax.Precision.HIGHEST
leja_order = (0, 7, 3, 5, 2, 6, 1, 4)
spread_scale = 6.5

def newton_shifts():
    return [13.125 + 12.875 * math.cos(math.pi * (2 * position + 1) / 16.0) for position in leja_order]

def shift_table():
    shifts = newton_shifts()
    table = np.zeros((COLS, STEPS))
    for number in range(STEPS):
        table[number, number] = shifts[number]
        table[number + 1, number] = spread_scale
    return jnp.asarray(table, dtype=jnp.float32)

def column_qr(rows):
    count = rows.shape[0]
    basis = jnp.zeros_like(rows)
    factor = jnp.zeros((count, count), jnp.float32)
    for j in range(count):
        vector = rows[j]
        first = jnp.dot(basis, vector, precision=HIGH)
        vector = vector - jnp.dot(first, basis, precision=HIGH)
        second = jnp.dot(basis, vector, precision=HIGH)
        vector = vector - jnp.dot(second, basis, precision=HIGH)
        length = jnp.sqrt(jnp.dot(vector, vector, precision=HIGH) + 1e-12)
        basis = basis.at[j].set(vector / length)
        factor = factor.at[:, j].set(first + second)
        factor = factor.at[j, j].set(length)
    return (basis, factor)

def back_substitute(tri, coeff):
    count = tri.shape[0]
    solved = [None] * count
    for i in range(count - 1, -1, -1):
        total = coeff[i]
        for k in range(i + 1, count):
            total = total - tri[i, k] * solved[k]
        solved[i] = total / tri[i, i]
    return jnp.stack(solved)

def small_solve(factor):
    table = shift_table()
    hess = jnp.dot(factor, table, precision=HIGH)
    qrows, tri = column_qr(hess.T)
    target = factor[:, 0]
    coeff = jnp.dot(qrows, target, precision=HIGH)
    weights = back_substitute(tri, coeff)
    miss = target - jnp.dot(hess, weights, precision=HIGH)
    unit = jnp.zeros((COLS,), jnp.float32).at[0].set(1.0)
    mixing = unit - jnp.dot(table, weights, precision=HIGH)
    return (weights, jnp.sqrt(jnp.sum(miss * miss)), mixing)

def operate(field, conduct, storage):
    field_pad = jnp.pad(field, 1)
    coef_pad = jnp.pad(conduct, 1)
    result = storage * field
    moves = [(2, None, 1, -1, 1, -1), (0, -2, 1, -1, 1, -1), (1, -1, 2, None, 1, -1), (1, -1, 0, -2, 1, -1), (1, -1, 1, -1, 2, None), (1, -1, 1, -1, 0, -2)]
    for move in moves:
        where = (slice(move[0], move[1]), slice(move[2], move[3]), slice(move[4], move[5]))
        result = result + 0.5 * (conduct + coef_pad[where]) * (field - field_pad[where])
    return result

def reference(source, conduct, storage):
    shifts = newton_shifts()
    basis = [source]
    current = source
    for number in range(STEPS):
        current = (operate(current, conduct, storage) - shifts[number] * current) / spread_scale
        basis.append(current)
    stacked = jnp.stack(basis)
    _, factor = column_qr(stacked.reshape(COLS, -1))
    weights, resid, mixing = small_solve(factor)
    correction = jnp.tensordot(weights, stacked[:STEPS], axes=1, precision=HIGH)
    remainder = jnp.tensordot(mixing, stacked, axes=1, precision=HIGH)
    return (correction, remainder, factor, resid)
```

```python
import math

import jax
import jax.numpy as jnp
from jax import lax
from jax.experimental import pallas as pl
from jax.experimental.pallas import tpu as pltpu
from jax.sharding import PartitionSpec as P

STEPS = 8
COLS = 9
HALO = 8

leja_order = (0, 7, 3, 5, 2, 6, 1, 4)
spread_scale = 6.5
MIB = 1024 * 1024


def newton_shifts():
    return [
        13.125 + 12.875 * math.cos(math.pi * (2 * position + 1) / 16.0) for position in leja_order
    ]


def is_odd(axis):
    return lax.rem(lax.axis_index(axis), 2) == 1


def exchange(first, second, axis):
    size = lax.axis_size(axis)
    inner = [(i, i ^ 1) for i in range(size)]
    outer = [(i, (((i + 1) % size ^ 1) - 1) % size) for i in range(size)]
    return lax.ppermute(first, axis, inner), lax.ppermute(second, axis, outer)


def vmem_spec(count):
    return [pl.BlockSpec(memory_space=pltpu.VMEM)] * count


def edge_kernel(source, conduct, storage, inner, outer):
    odd = is_odd("narrow")
    width = source.shape[1]

    def fill(low, high):
        for k, ref in enumerate((source, conduct, storage)):
            low[k] = ref[:, 0:HALO, :]
            high[k] = ref[:, width - HALO : width, :]

    @pl.when(odd)
    def _():
        fill(inner, outer)

    @pl.when(jnp.logical_not(odd))
    def _():
        fill(outer, inner)


def edges(source, conduct, storage):
    size_x, _, size_z = source.shape
    shape = jax.ShapeDtypeStruct((3, size_x, HALO, size_z), jnp.float32)
    return pl.pallas_call(
        edge_kernel,
        out_shape=(shape, shape),
        in_specs=vmem_spec(3),
        out_specs=tuple(vmem_spec(2)),
        compiler_params=pltpu.CompilerParams(vmem_limit_bytes=8 * MIB),
        name="edges",
    )(source, conduct, storage)


def widen_kernel(last, source, conduct, storage, inner, outer, near, far):
    odd_n, odd_w = is_odd("narrow"), is_odd("wide")
    place = lax.axis_index("narrow")
    keep_low = jnp.where(place == 0, 0.0, 1.0)
    keep_high = jnp.where(place == last, 0.0, 1.0)
    size_x, width, _ = source.shape
    half = size_x // 2

    def fill(low_rows, high_rows, low_half, high_half):
        for k, ref in enumerate((source, conduct, storage)):
            for part, out in ((0, low_half), (1, high_half)):
                cells = slice(part * half, (part + 1) * half)
                out[k, :, 0:HALO, :] = low_rows[k, cells] * keep_low
                out[k, :, HALO : HALO + width, :] = ref[cells]
                out[k, :, HALO + width :, :] = high_rows[k, cells] * keep_high

    for flag_n in (False, True):
        for flag_w in (False, True):

            @pl.when(jnp.logical_and(odd_n == flag_n, odd_w == flag_w))
            def _(flag_n=flag_n, flag_w=flag_w):
                rows = (inner, outer) if flag_n else (outer, inner)
                halves = (near, far) if flag_w else (far, near)
                fill(*rows, *halves)


def widen(source, conduct, storage, inner, outer):
    size_x, width, size_z = source.shape
    shape = jax.ShapeDtypeStruct((3, size_x // 2, width + 2 * HALO, size_z), jnp.float32)
    last = lax.axis_size("narrow") - 1
    return pl.pallas_call(
        lambda *refs: widen_kernel(last, *refs),
        out_shape=(shape, shape),
        in_specs=vmem_spec(5),
        out_specs=tuple(vmem_spec(2)),
        compiler_params=pltpu.CompilerParams(vmem_limit_bytes=8 * MIB),
        name="widen",
    )(source, conduct, storage, inner, outer)


def total(x):
    return jnp.sum(jnp.sum(x, axis=0, keepdims=True), axis=1, keepdims=True)


def basis_kernel(
    last, near, far, inner, outer, basis, rows_out,
    field_a, field_b, cond, diag, face_x, face_y, face_yp, face_z, face_zp, work,
):
    odd_w = is_odd("wide")
    place_w, place_n = lax.axis_index("wide"), lax.axis_index("narrow")
    keep_left = jnp.where(place_w == 0, 0.0, 1.0)
    keep_right = jnp.where(place_w == last[0], 0.0, 1.0)
    keep_low = jnp.where(place_n == 0, 0.0, 1.0)
    keep_high = jnp.where(place_n == last[1], 0.0, 1.0)
    long_x, long_y, size_z = cond.shape
    size_x, size_y = long_x - 2 * HALO, long_y - 2 * HALO
    shifts = newton_shifts()
    mid = pl.ds(HALO, long_y)

    def place(parts):
        at = 0
        for part, keep in zip(parts, (keep_left, None, None, keep_right)):
            planes = part.shape[1]
            for k, out in enumerate((field_a, cond, diag)):
                rows = mid if k == 0 else slice(None)
                value = part[k]
                out[at : at + planes, rows, :] = value if keep is None else value * keep
            at += planes

    @pl.when(odd_w)
    def _():
        place((inner, near, far, outer))

    @pl.when(jnp.logical_not(odd_w))
    def _():
        place((outer, far, near, inner))

    lane = lax.broadcasted_iota(jnp.int32, (long_y, size_z), 1)
    row = lax.broadcasted_iota(jnp.int32, (long_y, size_z), 0)
    unit = 1.0 / spread_scale
    half = 0.5 * unit
    mask_z = jnp.where(lane == 0, 0.0, half)
    mask_zp = jnp.where(lane == size_z - 1, 0.0, half)
    mask_y = jnp.where(row == HALO, keep_low, jnp.where(row == HALO + size_y, keep_high, 1.0))
    mask_yp = jnp.where(
        row == HALO - 1, keep_low, jnp.where(row == HALO + size_y - 1, keep_high, 1.0)
    )

    def coefficients(x, _):
        here = cond[x]
        left = half * (here + cond[x - 1])
        right = half * (here + cond[x + 1])
        down = jnp.concatenate([here[:1], here[:-1]], axis=0)
        up = jnp.concatenate([here[1:], here[-1:]], axis=0)
        low, high = half * (here + down), half * (here + up)
        back = pltpu.roll(here, 1, 1)
        front = pltpu.roll(here, size_z - 1, 1)
        z_low = mask_z * (here + back)
        z_high = mask_zp * (here + front)
        z_all = jnp.where(lane == 0, half * here, z_low) + jnp.where(
            lane == size_z - 1, half * here, z_high
        )
        face_x[x] = left
        face_y[x] = low * mask_y
        face_yp[x] = high * mask_yp
        face_z[x] = z_low
        face_zp[x] = z_high
        diag[x] = unit * diag[x] + ((left + right) + (low + high) + z_all)
        return 0

    lax.fori_loop(1, long_x - 1, coefficients, 0)
    face_x[HALO] = face_x[HALO] * keep_left
    face_x[HALO + size_x] = (
        half * (cond[HALO + size_x - 1] + cond[HALO + size_x]) * keep_right
    )
    face_x[long_x - 1] = half * (cond[long_x - 2] + cond[long_x - 1])

    def step(number, read, write):
        theta = shifts[number] * unit
        final = number == STEPS - 1
        low, count = (HALO, size_y) if final else (0, long_y)
        rows = pl.ds(low, count)

        def plane(x, keep):
            here = read[x, pl.ds(HALO + low, count), :]
            below = read[x, pl.ds(HALO + low - 1, count), :]
            above = read[x, pl.ds(HALO + low + 1, count), :]
            beside = (
                face_x[x + 1, rows, :] * read[x + 1, pl.ds(HALO + low, count), :]
                + face_x[x, rows, :] * read[x - 1, pl.ds(HALO + low, count), :]
            )
            across = face_yp[x, rows, :] * above + face_y[x, rows, :] * below
            along = face_zp[x, rows, :] * pltpu.roll(here, size_z - 1, 1) + face_z[
                x, rows, :
            ] * pltpu.roll(here, 1, 1)
            value = (diag[x, rows, :] - theta) * here - (beside + across + along)
            if not final:
                write[x, pl.ds(HALO, long_y), :] = value
            if keep:
                own = value if final else value[HALO : HALO + size_y]
                basis[number, x - HALO] = own

        def run(start, stop, keep):
            def body(x, _):
                plane(x, keep)
                return 0

            if stop > start:
                lax.fori_loop(start, stop, body, 0)

        run(number + 1, HALO, False)
        run(HALO, HALO + size_x, True)
        run(HALO + size_x, long_x - 1 - number, False)

    fields = (field_a, field_b)
    for ref in fields:
        for x in range(long_x):
            ref[x, 0:HALO, :] = jnp.zeros((HALO, size_z), jnp.float32)
            ref[x, HALO + long_y :, :] = jnp.zeros((HALO, size_z), jnp.float32)
    work[0] = field_a[HALO : HALO + size_x, pl.ds(2 * HALO, size_y), :]
    for number in range(STEPS):
        step(number, fields[number % 2], fields[(number + 1) % 2])

    def fold(product):
        parts = [product[8 * t : 8 * t + 8] for t in range(size_y // 8)]
        while len(parts) > 1:
            parts = [a + b for a, b in zip(parts[::2], parts[1::2])]
        return parts[0]

    zero = jnp.zeros((8, size_z), jnp.float32)

    def first_dots(x, sums):
        columns = [work[0, x]] + [basis[j, x] for j in range(STEPS)]
        return tuple(s + fold(columns[0] * c) for s, c in zip(sums, columns))

    sums = lax.fori_loop(0, size_x, first_dots, (zero,) * COLS)
    dots = [total(s) for s in sums]
    index = lax.broadcasted_iota(jnp.int32, (1, 128), 1)
    packed = jnp.zeros((1, 128), jnp.float32)
    for k in range(COLS):
        length = jnp.sqrt(dots[0])
        inverse = jnp.where(dots[0] > 0.0, 1.0 / length, 0.0)
        ratio = [d * inverse * inverse for d in dots]
        for j in range(k, COLS):
            entry = length if j == k else dots[j - k] * inverse
            packed = jnp.where(index == 8 * j + k, entry, packed)
        if k == COLS - 1:
            break

        def sweep(x, sums, k=k, ratio=ratio):
            pivot = work[k, x]
            columns = []
            for j in range(k + 1, COLS):
                old = basis[j - 1, x] if k == 0 else work[j, x]
                new = old - ratio[j - k] * pivot
                work[j, x] = new
                columns.append(new)
            return tuple(s + fold(columns[0] * c) for s, c in zip(sums, columns))

        sums = lax.fori_loop(0, size_x, sweep, (zero,) * (COLS - 1 - k))
        dots = [total(s) for s in sums]
    rows_out[...] = jnp.broadcast_to(packed, rows_out.shape)


def basis_and_factor(near, far, inner, outer):
    _, half, long_y, size_z = near.shape
    size_x, size_y = 2 * half, long_y - 2 * HALO
    long_x = size_x + 2 * HALO
    devices = lax.axis_size("wide") * lax.axis_size("narrow")
    last = (lax.axis_size("wide") - 1, lax.axis_size("narrow") - 1)
    field = pltpu.VMEM((long_x, long_y + 2 * HALO, size_z), jnp.float32)
    plain = pltpu.VMEM((long_x, long_y, size_z), jnp.float32)
    return pl.pallas_call(
        lambda *refs: basis_kernel(last, *refs),
        out_shape=(
            jax.ShapeDtypeStruct((STEPS, size_x, size_y, size_z), jnp.float32),
            jax.ShapeDtypeStruct((devices, 128), jnp.float32),
        ),
        in_specs=vmem_spec(4),
        out_specs=tuple(vmem_spec(2)),
        scratch_shapes=[field, field] + [plain] * 7
        + [pltpu.VMEM((COLS, size_x, size_y, size_z), jnp.float32)],
        compiler_params=pltpu.CompilerParams(vmem_limit_bytes=32 * MIB),
        name="basis_and_factor",
    )(near, far, inner, outer)


def split(x):
    big = x * 4097.0
    high = big - (big - x)
    return high, x - high


def two_sum(a, b):
    s = a + b
    t = s - a
    return s, (a - (s - t)) + (b - t)


def small_solve(factor):
    shifts = newton_shifts()
    null = [1.0]
    for theta in shifts:
        null.append(-theta / spread_scale * null[-1])
    inverse = [1.0 / factor[(i, i)] for i in range(COLS)]

    left = [jnp.full((1, 1), w, jnp.float32) for w in null]
    normal = []
    for i in range(COLS):
        normal.append(left[i] * inverse[i])
        for j in range(i + 1, COLS):
            left[j] = left[j] - factor[(i, j)] * normal[i]
    square = normal[0] * normal[0]
    for i in range(1, COLS):
        square = square + normal[i] * normal[i]
    target = [entry / square for entry in normal]

    def back(right):
        right, solved = list(right), [None] * COLS
        for j in range(COLS - 1, -1, -1):
            solved[j] = right[j] * inverse[j]
            for i in range(j):
                right[i] = right[i] - factor[(i, j)] * solved[j]
        return solved

    z = back(target)
    z_parts = [split(entry) for entry in z]
    missing = []
    for i in range(COLS):
        high, low = target[i], None
        for j in range(i, COLS):
            (ah, al), (bh, bl) = split(factor[(i, j)]), z_parts[j]
            product = factor[(i, j)] * z[j]
            error = ((ah * bh - product) + ah * bl + al * bh) + al * bl
            high, carry = two_sum(high, -product)
            carry = carry - error
            low = carry if low is None else low + carry
        missing.append(high + low)
    z = [a + b for a, b in zip(z, back(missing))]

    y = [None] * STEPS
    for j in range(STEPS, 0, -1):
        right = -z[j]
        if j < STEPS:
            right = right - shifts[j] * y[j]
        y[j - 1] = right * (1.0 / spread_scale)
    return y, 1.0 / jnp.sqrt(square), z


def combine_kernel(source, basis, rows, correction, remainder, upper, norm):
    stacked = rows[...].T
    tops = [stacked[8 * j : 8 * j + 8] for j in range(COLS)]
    tail = stacked[8 * COLS : 8 * COLS + 8]
    sublane = lax.broadcasted_iota(jnp.int32, (8, 128), 0)
    tail = jnp.where(sublane == 0, tail, 0.0)
    factor = {}
    for k in range(COLS):
        square = tops[k] * tops[k]
        if k == COLS - 1:
            square = square + tail * tail
        dots = [total(square)] + [total(tops[k] * tops[j]) for j in range(k + 1, COLS)]
        ridge = dots[0] + 1e-12
        length = jnp.sqrt(ridge)
        again = 2.0 - dots[0] / ridge
        factor[(k, k)] = length
        for j in range(k + 1, COLS):
            factor[(k, j)] = dots[j - k] / length * again
            tops[j] = tops[j] - (dots[j - k] / ridge * again) * tops[k]

    y, size, z = small_solve(factor)

    line = lax.broadcasted_iota(jnp.int32, (16, 128), 0)
    lane = lax.broadcasted_iota(jnp.int32, (16, 128), 1)
    table = jnp.zeros((16, 128), jnp.float32)
    for (i, j), entry in factor.items():
        table = jnp.where(jnp.logical_and(line == i, lane == j), entry, table)
    upper[...] = table[:COLS, :COLS]
    norm[...] = size

    def combine(x, _):
        here = source[x]
        first, second = y[0] * here, z[0] * here
        for j in range(1, COLS):
            here = basis[j - 1, x]
            if j < STEPS:
                first = first + y[j] * here
            second = second + z[j] * here
        correction[x] = first
        remainder[x] = second
        return 0

    lax.fori_loop(0, source.shape[0], combine, 0)


def combine(source, basis, rows):
    block = jax.ShapeDtypeStruct(source.shape, jnp.float32)
    return pl.pallas_call(
        combine_kernel,
        out_shape=(
            block,
            block,
            jax.ShapeDtypeStruct((COLS, COLS), jnp.float32),
            jax.ShapeDtypeStruct((1, 1), jnp.float32),
        ),
        in_specs=vmem_spec(3),
        out_specs=tuple(vmem_spec(4)),
        compiler_params=pltpu.CompilerParams(vmem_limit_bytes=8 * MIB),
        name="combine",
    )(source, basis, rows)


def on_device(source, conduct, storage):
    rows = exchange(*edges(source, conduct, storage), "narrow")
    near, far = widen(source, conduct, storage, *rows)
    planes = exchange(near, far, "wide")
    basis, packed = basis_and_factor(near, far, *planes)
    gathered = lax.all_to_all(packed, ("wide", "narrow"), 0, 0, tiled=True)
    correction, remainder, factor, resid = combine(source, basis, gathered)
    return correction, remainder, factor, resid[0, 0]


def solution(mesh):
    spec = P("wide", "narrow", None)
    return jax.shard_map(
        on_device,
        mesh=mesh,
        in_specs=(spec, spec, spec),
        out_specs=(spec, spec, P(), P()),
        check_vma=False,
    )
```

```python
import math

import jax
import jax.numpy as jnp
from jax import lax
from jax.experimental import pallas as pl
from jax.experimental.pallas import tpu as pltpu
from jax.sharding import PartitionSpec as P

STEPS = 8
COLS = 9
HALO = 8

leja_order = (0, 7, 3, 5, 2, 6, 1, 4)
spread_scale = 6.5
MIB = 1024 * 1024


def newton_shifts():
    return [
        13.125 + 12.875 * math.cos(math.pi * (2 * position + 1) / 16.0) for position in leja_order
    ]


def is_odd(axis):
    return lax.rem(lax.axis_index(axis), 2) == 1


def exchange(first, second, axis):
    size = lax.axis_size(axis)
    inner = [(i, i ^ 1) for i in range(size)]
    outer = [(i, (((i + 1) % size ^ 1) - 1) % size) for i in range(size)]
    return lax.ppermute(first, axis, inner), lax.ppermute(second, axis, outer)


def vmem_spec(count):
    return [pl.BlockSpec(memory_space=pltpu.VMEM)] * count


def edge_kernel(source, conduct, storage, inner, outer, own, sems):
    odd = is_odd("narrow")
    width = source.shape[1]

    def fill(low, high):
        copies = []
        for k, ref in enumerate((source, conduct, storage)):
            for side, (at, out) in enumerate(((0, low), (width - HALO, high))):
                copies.append(
                    pltpu.make_async_copy(
                        ref.at[:, pl.ds(at, HALO), :], out.at[k], sems.at[2 * k + side]
                    )
                )
            copies.append(pltpu.make_async_copy(ref, own.at[k], sems.at[6 + k]))
        for copy in copies:
            copy.start()
        for copy in copies:
            copy.wait()

    @pl.when(odd)
    def _():
        fill(inner, outer)

    @pl.when(jnp.logical_not(odd))
    def _():
        fill(outer, inner)


def edges(source, conduct, storage):
    size_x, _, size_z = source.shape
    shape = jax.ShapeDtypeStruct((3, size_x, HALO, size_z), jnp.float32)
    whole = jax.ShapeDtypeStruct((3, *source.shape), jnp.float32)
    return pl.pallas_call(
        edge_kernel,
        out_shape=(shape, shape, whole),
        in_specs=[pl.BlockSpec(memory_space=pltpu.HBM)] * 3,
        out_specs=tuple(vmem_spec(3)),
        scratch_shapes=[pltpu.SemaphoreType.DMA((9,))],
        compiler_params=pltpu.CompilerParams(vmem_limit_bytes=8 * MIB),
        name="edges",
    )(*(pltpu.with_memory_space_constraint(x, pltpu.HBM) for x in (source, conduct, storage)))


def widen_kernel(last, own, inner, outer, near, far):
    odd_n, odd_w = is_odd("narrow"), is_odd("wide")
    place = lax.axis_index("narrow")
    keep_low = jnp.where(place == 0, 0.0, 1.0)
    keep_high = jnp.where(place == last, 0.0, 1.0)
    _, size_x, width, _ = own.shape
    half = size_x // 2

    def fill(low_rows, high_rows, low_half, high_half):
        for k in range(3):
            for part, out in ((0, low_half), (1, high_half)):
                cells = slice(part * half, (part + 1) * half)
                out[k, :, 0:HALO, :] = low_rows[k, cells] * keep_low
                out[k, :, HALO : HALO + width, :] = own[k, cells]
                out[k, :, HALO + width :, :] = high_rows[k, cells] * keep_high

    for flag_n in (False, True):
        for flag_w in (False, True):

            @pl.when(jnp.logical_and(odd_n == flag_n, odd_w == flag_w))
            def _(flag_n=flag_n, flag_w=flag_w):
                rows = (inner, outer) if flag_n else (outer, inner)
                halves = (near, far) if flag_w else (far, near)
                fill(*rows, *halves)


def widen(own, inner, outer):
    _, size_x, width, size_z = own.shape
    shape = jax.ShapeDtypeStruct((3, size_x // 2, width + 2 * HALO, size_z), jnp.float32)
    last = lax.axis_size("narrow") - 1
    return pl.pallas_call(
        lambda *refs: widen_kernel(last, *refs),
        out_shape=(shape, shape),
        in_specs=vmem_spec(3),
        out_specs=tuple(vmem_spec(2)),
        compiler_params=pltpu.CompilerParams(vmem_limit_bytes=8 * MIB),
        name="widen",
    )(own, inner, outer)


def total(x):
    return jnp.sum(jnp.sum(x, axis=0, keepdims=True), axis=1, keepdims=True)


def basis_kernel(
    last, long_y, near, far, inner, outer, basis, rows_out,
    field, cond, diag, face_x, face_y, face_yp, face_z, face_zp,
    back_a, front_a, back_b, front_b, work,
):
    odd_w = is_odd("wide")
    place_w, place_n = lax.axis_index("wide"), lax.axis_index("narrow")
    keep_left = jnp.where(place_w == 0, 0.0, 1.0)
    keep_right = jnp.where(place_w == last[0], 0.0, 1.0)
    keep_low = jnp.where(place_n == 0, 0.0, 1.0)
    keep_high = jnp.where(place_n == last[1], 0.0, 1.0)
    size_z = field.shape[1]
    long_x = field.shape[0] // long_y
    size_x, size_y = long_x - 2 * HALO, long_y - 2 * HALO
    shifts = newton_shifts()

    def at(x, count=long_y, first=0):
        start = x * long_y + first
        if not isinstance(x, int) and first % 8 == 0:
            start = pl.multiple_of(start, 8)
        return pl.ds(start, count)

    def place(parts):
        start = 0
        for part, keep in zip(parts, (keep_left, None, None, keep_right)):
            rows = part.shape[1]
            for k, (out, skip) in enumerate(((field, 0), (cond, long_y), (diag, 0))):
                value = part[k]
                out[pl.ds(start + skip, rows), :] = value if keep is None else value * keep
            start += rows

    @pl.when(odd_w)
    def _():
        place((inner, near, far, outer))

    @pl.when(jnp.logical_not(odd_w))
    def _():
        place((outer, far, near, inner))

    empty = jnp.zeros((long_y, size_z), jnp.float32)
    cond[at(0), :] = empty
    cond[at(long_x + 1), :] = empty

    lane = lax.broadcasted_iota(jnp.int32, (long_y, size_z), 1)
    row = lax.broadcasted_iota(jnp.int32, (long_y, size_z), 0)
    unit = 1.0 / spread_scale
    half = 0.5 * unit
    mask_y = jnp.where(row == HALO, keep_low, jnp.where(row == HALO + size_y, keep_high, 1.0))
    mask_yp = jnp.where(
        row == HALO - 1, keep_low, jnp.where(row == HALO + size_y - 1, keep_high, 1.0)
    )

    def turn(value):
        return (
            jnp.where(lane == 0, 0.0, pltpu.roll(value, 1, 1)),
            jnp.where(lane == size_z - 1, 0.0, pltpu.roll(value, size_z - 1, 1)),
        )

    def turn_start(x):
        here = field[at(x), :]
        back_a[at(x), :] = pltpu.roll(here, 1, 1)
        front_a[at(x), :] = pltpu.roll(here, size_z - 1, 1)
        back, front = turn(cond[at(x + 1), :])
        back_b[at(x), :] = back
        front_b[at(x), :] = front

    def coefficients(x):
        here = cond[at(x + 1), :]
        left = half * (here + cond[at(x), :])
        right = half * (here + cond[at(x + 2), :])
        low = half * (here + cond[at(x + 1, long_y, -1), :])
        high = half * (here + cond[at(x + 1, long_y, 1), :])
        z_low = half * (here + back_b[at(x), :])
        z_high = half * (here + front_b[at(x), :])
        face_x[at(x), :] = left
        face_y[at(x), :] = low * mask_y
        face_yp[at(x), :] = high * mask_yp
        face_z[at(x), :] = jnp.where(lane == 0, 0.0, z_low)
        face_zp[at(x), :] = jnp.where(lane == size_z - 1, 0.0, z_high)
        diag[at(x), :] = unit * diag[at(x), :] + ((left + right) + (low + high) + (z_low + z_high))

    group = 4

    def start_group(g, _):
        for i in range(group):
            coefficients((g - 1) * group + i)
        for i in range(group):
            turn_start(g * group + i)
        return 0

    for i in range(group):
        turn_start(i)
    lax.fori_loop(1, long_x // group, start_group, 0)
    for i in range(group):
        coefficients(long_x - group + i)
    face_x[at(HALO), :] = face_x[at(HALO), :] * keep_left
    face_x[at(HALO + size_x), :] = face_x[at(HALO + size_x), :] * keep_right

    def step(number, read, back, front, write, next_back, next_front):
        theta = shifts[number] * unit
        final = number == STEPS - 1
        low, count = (HALO, size_y) if final else (0, long_y)

        def plane(x):
            rows = at(x, count, low)
            here = read[rows, :]
            beside = (
                face_x[at(x + 1, count, low), :] * read[at(x + 1, count, low), :]
                + face_x[rows, :] * read[at(x - 1, count, low), :]
            )
            across = (
                face_yp[rows, :] * read[at(x, count, low + 1), :]
                + face_y[rows, :] * read[at(x, count, low - 1), :]
            )
            along = face_zp[rows, :] * front[rows, :] + face_z[rows, :] * back[rows, :]
            write[rows, :] = (diag[rows, :] - theta) * here - (beside + across + along)

        def turn_plane(x):
            if not final:
                here = write[at(x), :]
                next_back[at(x), :] = pltpu.roll(here, 1, 1)
                next_front[at(x), :] = pltpu.roll(here, size_z - 1, 1)

        start, stop = number + 1, long_x - 1 - number
        head = (stop - start) % group or group
        for x in range(start, start + head):
            plane(x)
        for x in range(start + 1, start + head):
            turn_plane(x)
        begin = start + head
        for x in range(begin, begin + group):
            plane(x)

        def body(g, _):
            x = begin + g * group
            for i in range(group):
                turn_plane(x - group + i)
            for i in range(group):
                plane(x + i)
            return 0

        lax.fori_loop(1, (stop - begin) // group, body, 0)
        for x in range(stop - group, stop - 1):
            turn_plane(x)

    turned = ((back_a, front_a), (back_b, front_b))
    for number in range(STEPS):
        read = field if number == 0 else basis.at[number - 1]
        step(number, read, *turned[number % 2], basis.at[number], *turned[(number + 1) % 2])

    def own(x):
        return at(x + HALO, size_y, HALO)

    def fold(product):
        parts = [product[8 * t : 8 * t + 8] for t in range(size_y // 8)]
        while len(parts) > 1:
            parts = [a + b for a, b in zip(parts[::2], parts[1::2])]
        return parts[0]

    zero = jnp.zeros((8, size_z), jnp.float32)

    def first_dots(x, sums):
        columns = [field[own(x), :]] + [basis[j, own(x), :] for j in range(STEPS)]
        return tuple(s + fold(columns[0] * c) for s, c in zip(sums, columns))

    sums = lax.fori_loop(0, size_x, first_dots, (zero,) * COLS)
    dots = [total(s) for s in sums]
    index = lax.broadcasted_iota(jnp.int32, (1, 128), 1)
    packed = jnp.zeros((1, 128), jnp.float32)
    for k in range(COLS):
        length = jnp.sqrt(dots[0])
        inverse = jnp.where(dots[0] > 0.0, 1.0 / length, 0.0)
        ratio = [d * inverse * inverse for d in dots]
        for j in range(k, COLS):
            entry = length if j == k else dots[j - k] * inverse
            packed = jnp.where(index == 8 * j + k, entry, packed)
        if k == COLS - 1:
            break

        def sweep(x, sums, k=k, ratio=ratio):
            pivot = field[own(x), :] if k == 0 else work[k, x]
            columns = []
            for j in range(k + 1, COLS):
                old = basis[j - 1, own(x), :] if k == 0 else work[j, x]
                new = old - ratio[j - k] * pivot
                work[j, x] = new
                columns.append(new)
            return tuple(s + fold(columns[0] * c) for s, c in zip(sums, columns))

        sums = lax.fori_loop(0, size_x, sweep, (zero,) * (COLS - 1 - k))
        dots = [total(s) for s in sums]
    rows_out[...] = jnp.broadcast_to(packed, rows_out.shape)


def basis_and_factor(near, far, inner, outer):
    _, half, long_y, size_z = near.shape
    size_x, size_y = 2 * half, long_y - 2 * HALO
    long_x = size_x + 2 * HALO
    devices = lax.axis_size("wide") * lax.axis_size("narrow")
    last = (lax.axis_size("wide") - 1, lax.axis_size("narrow") - 1)
    flat = lambda x: x.reshape(3, half * long_y, size_z)
    planes = lambda count: pltpu.VMEM((count * long_y, size_z), jnp.float32)
    return pl.pallas_call(
        lambda *refs: basis_kernel(last, long_y, *refs),
        out_shape=(
            jax.ShapeDtypeStruct((STEPS, long_x * long_y, size_z), jnp.float32),
            jax.ShapeDtypeStruct((devices, 128), jnp.float32),
        ),
        in_specs=vmem_spec(4),
        out_specs=tuple(vmem_spec(2)),
        scratch_shapes=[planes(long_x), planes(long_x + 2)] + [planes(long_x)] * 10
        + [pltpu.VMEM((COLS, size_x, size_y, size_z), jnp.float32)],
        compiler_params=pltpu.CompilerParams(vmem_limit_bytes=28 * MIB),
        name="basis_and_factor",
    )(flat(near), flat(far), flat(inner), flat(outer))


def split(x):
    big = x * 4097.0
    high = big - (big - x)
    return high, x - high


def two_sum(a, b):
    s = a + b
    t = s - a
    return s, (a - (s - t)) + (b - t)


def small_solve(factor):
    shifts = newton_shifts()
    null = [1.0]
    for theta in shifts:
        null.append(-theta / spread_scale * null[-1])
    inverse = [1.0 / factor[(i, i)] for i in range(COLS)]

    left = [jnp.full((1, 1), w, jnp.float32) for w in null]
    normal = []
    for i in range(COLS):
        normal.append(left[i] * inverse[i])
        for j in range(i + 1, COLS):
            left[j] = left[j] - factor[(i, j)] * normal[i]
    square = normal[0] * normal[0]
    for i in range(1, COLS):
        square = square + normal[i] * normal[i]
    target = [entry / square for entry in normal]

    def back(right):
        right, solved = list(right), [None] * COLS
        for j in range(COLS - 1, -1, -1):
            solved[j] = right[j] * inverse[j]
            for i in range(j):
                right[i] = right[i] - factor[(i, j)] * solved[j]
        return solved

    z = back(target)
    z_parts = [split(entry) for entry in z]
    missing = []
    for i in range(COLS):
        high, low = target[i], None
        for j in range(i, COLS):
            (ah, al), (bh, bl) = split(factor[(i, j)]), z_parts[j]
            product = factor[(i, j)] * z[j]
            error = ((ah * bh - product) + ah * bl + al * bh) + al * bl
            high, carry = two_sum(high, -product)
            carry = carry - error
            low = carry if low is None else low + carry
        missing.append(high + low)
    z = [a + b for a, b in zip(z, back(missing))]

    y = [None] * STEPS
    for j in range(STEPS, 0, -1):
        right = -z[j]
        if j < STEPS:
            right = right - shifts[j] * y[j]
        y[j - 1] = right * (1.0 / spread_scale)
    return y, 1.0 / jnp.sqrt(square), z


def combine_kernel(own, basis, rows, correction, remainder, upper, norm):
    stacked = rows[...].T
    tops = [stacked[8 * j : 8 * j + 8] for j in range(COLS)]
    tail = stacked[8 * COLS : 8 * COLS + 8]
    sublane = lax.broadcasted_iota(jnp.int32, (8, 128), 0)
    tail = jnp.where(sublane == 0, tail, 0.0)
    factor = {}
    for k in range(COLS):
        square = tops[k] * tops[k]
        if k == COLS - 1:
            square = square + tail * tail
        dots = [total(square)] + [total(tops[k] * tops[j]) for j in range(k + 1, COLS)]
        ridge = dots[0] + 1e-12
        length = jnp.sqrt(ridge)
        again = 2.0 - dots[0] / ridge
        factor[(k, k)] = length
        for j in range(k + 1, COLS):
            factor[(k, j)] = dots[j - k] / length * again
            tops[j] = tops[j] - (dots[j - k] / ridge * again) * tops[k]

    y, size, z = small_solve(factor)

    line = lax.broadcasted_iota(jnp.int32, (16, 128), 0)
    lane = lax.broadcasted_iota(jnp.int32, (16, 128), 1)
    table = jnp.zeros((16, 128), jnp.float32)
    for (i, j), entry in factor.items():
        table = jnp.where(jnp.logical_and(line == i, lane == j), entry, table)
    upper[...] = table[:COLS, :COLS]
    norm[...] = size

    _, size_x, size_y, _ = own.shape
    long_y = size_y + 2 * HALO

    def combine(x, _):
        here = own[0, x]
        first, second = y[0] * here, z[0] * here
        for j in range(1, COLS):
            here = basis[j - 1, pl.ds(pl.multiple_of((x + HALO) * long_y + HALO, 8), size_y), :]
            if j < STEPS:
                first = first + y[j] * here
            second = second + z[j] * here
        correction[x] = first
        remainder[x] = second
        return 0

    lax.fori_loop(0, size_x, combine, 0)


def combine(own, basis, rows):
    block = jax.ShapeDtypeStruct(own.shape[1:], jnp.float32)
    return pl.pallas_call(
        combine_kernel,
        out_shape=(
            block,
            block,
            jax.ShapeDtypeStruct((COLS, COLS), jnp.float32),
            jax.ShapeDtypeStruct((1, 1), jnp.float32),
        ),
        in_specs=vmem_spec(3),
        out_specs=tuple(vmem_spec(4)),
        compiler_params=pltpu.CompilerParams(vmem_limit_bytes=8 * MIB),
        name="combine",
    )(own, basis, rows)


def on_device(source, conduct, storage):
    inner, outer, own = edges(source, conduct, storage)
    near, far = widen(own, *exchange(inner, outer, "narrow"))
    planes = exchange(near, far, "wide")
    basis, packed = basis_and_factor(near, far, *planes)
    gathered = lax.all_to_all(packed, ("wide", "narrow"), 0, 0, tiled=True)
    correction, remainder, factor, resid = combine(own, basis, gathered)
    return correction, remainder, factor, resid[0, 0]


def solution(mesh):
    spec = P("wide", "narrow", None)
    return jax.shard_map(
        on_device,
        mesh=mesh,
        in_specs=(spec, spec, spec),
        out_specs=(spec, spec, P(), P()),
        check_vma=False,
    )
```

```python
import math

import jax
import jax.numpy as jnp
from jax import lax
from jax.experimental import pallas as pl
from jax.experimental.pallas import tpu as pltpu
from jax.sharding import PartitionSpec as P

STEPS = 8
COLS = 9
HALO = 8

leja_order = (0, 7, 3, 5, 2, 6, 1, 4)
spread_scale = 6.5
MIB = 1024 * 1024


def newton_shifts():
    return [
        13.125 + 12.875 * math.cos(math.pi * (2 * position + 1) / 16.0) for position in leja_order
    ]


def is_odd(axis):
    return lax.rem(lax.axis_index(axis), 2) == 1


def exchange(first, second, axis):
    size = lax.axis_size(axis)
    inner = [(i, i ^ 1) for i in range(size)]
    outer = [(i, (((i + 1) % size ^ 1) - 1) % size) for i in range(size)]
    return lax.ppermute(first, axis, inner), lax.ppermute(second, axis, outer)


def vmem_spec(count):
    return [pl.BlockSpec(memory_space=pltpu.VMEM)] * count


def edge_kernel(source, conduct, storage, inner, outer, near, far, sems):
    odd_n, odd_w = is_odd("narrow"), is_odd("wide")
    size_x, width, _ = source.shape
    half = size_x // 2

    def copies(low, high, first, second):
        result = []
        for k, ref in enumerate((source, conduct, storage)):
            result += [
                pltpu.make_async_copy(ref.at[:, pl.ds(0, HALO), :], low.at[k], sems.at[k]),
                pltpu.make_async_copy(
                    ref.at[:, pl.ds(width - HALO, HALO), :], high.at[k], sems.at[3 + k]
                ),
                pltpu.make_async_copy(ref.at[pl.ds(0, half)], first.at[k], sems.at[6 + k]),
                pltpu.make_async_copy(ref.at[pl.ds(half, half)], second.at[k], sems.at[9 + k]),
            ]
        return result

    for flag_n in (False, True):
        for flag_w in (False, True):

            @pl.when(jnp.logical_and(odd_n == flag_n, odd_w == flag_w))
            def _(flag_n=flag_n, flag_w=flag_w):
                rows = (inner, outer) if flag_n else (outer, inner)
                halves = (near, far) if flag_w else (far, near)
                every = copies(*rows, *halves)
                for copy in every:
                    copy.start()
                for copy in every:
                    copy.wait()


def edges(source, conduct, storage):
    size_x, width, size_z = source.shape
    rows = jax.ShapeDtypeStruct((3, size_x, HALO, size_z), jnp.float32)
    halves = jax.ShapeDtypeStruct((3, size_x // 2, width, size_z), jnp.float32)
    return pl.pallas_call(
        edge_kernel,
        out_shape=(rows, rows, halves, halves),
        in_specs=[pl.BlockSpec(memory_space=pltpu.HBM)] * 3,
        out_specs=tuple(vmem_spec(4)),
        scratch_shapes=[pltpu.SemaphoreType.DMA((12,))],
        compiler_params=pltpu.CompilerParams(vmem_limit_bytes=8 * MIB),
        name="edges",
    )(*(pltpu.with_memory_space_constraint(x, pltpu.HBM) for x in (source, conduct, storage)))


def corner_kernel(inner, outer, near, far):
    odd_n, odd_w = is_odd("narrow"), is_odd("wide")
    half = near.shape[1]
    row = lax.broadcasted_iota(jnp.int32, near.shape[2:], 0)

    def fill(low_rows, high_rows, low_half, high_half):
        for k in range(3):
            for p in range(half):
                low_half[k, p] = jnp.where(
                    row >= p + 1, low_rows[k, p], high_rows[k, half - 1 - p]
                )
                high_half[k, p] = jnp.where(
                    row >= half - p, low_rows[k, half + p], high_rows[k, 2 * half - 1 - p]
                )

    for flag_n in (False, True):
        for flag_w in (False, True):

            @pl.when(jnp.logical_and(odd_n == flag_n, odd_w == flag_w))
            def _(flag_n=flag_n, flag_w=flag_w):
                rows = (inner, outer) if flag_n else (outer, inner)
                halves = (near, far) if flag_w else (far, near)
                fill(*rows, *halves)


def corners(inner, outer):
    _, size_x, rows, size_z = inner.shape
    shape = jax.ShapeDtypeStruct((3, size_x // 2, rows, size_z), jnp.float32)
    return pl.pallas_call(
        corner_kernel,
        out_shape=(shape, shape),
        in_specs=vmem_spec(2),
        out_specs=tuple(vmem_spec(2)),
        compiler_params=pltpu.CompilerParams(vmem_limit_bytes=8 * MIB),
        name="corners",
    )(inner, outer)


def total(x):
    return jnp.sum(jnp.sum(x, axis=0, keepdims=True), axis=1, keepdims=True)


def basis_kernel(
    last, long_y, near, far, rows_inner, rows_outer, planes_inner, planes_outer,
    corner_inner, corner_outer, basis, rows_out,
    cond, diag, face_x, face_y, face_yp, face_z, face_zp,
    back_a, front_a, back_b, front_b, work,
):
    odd_w = is_odd("wide")
    place_w, place_n = lax.axis_index("wide"), lax.axis_index("narrow")
    keep_left = jnp.where(place_w == 0, 0.0, 1.0)
    keep_right = jnp.where(place_w == last[0], 0.0, 1.0)
    keep_low = jnp.where(place_n == 0, 0.0, 1.0)
    keep_high = jnp.where(place_n == last[1], 0.0, 1.0)
    field = basis.at[0]
    size_z = diag.shape[1]
    long_x = diag.shape[0] // long_y
    size_x, size_y = long_x - 2 * HALO, long_y - 2 * HALO
    shifts = newton_shifts()

    def at(x, count=long_y, first=0):
        start = x * long_y + first
        if not isinstance(x, int) and first % 8 == 0:
            start = pl.multiple_of(start, 8)
        return pl.ds(start, count)

    targets = ((field, 0), (cond, long_y), (diag, 0))

    def place_own(low, high, first, second):
        half = size_x // 2
        for k, (out, skip) in enumerate(targets):
            for p in range(size_x):
                start = skip + (HALO + p) * long_y
                out[pl.ds(start, HALO), :] = low[k, p] * keep_low
                own = first[k, p] if p < half else second[k, p - half]
                out[pl.ds(start + HALO, size_y), :] = own
                out[pl.ds(start + HALO + size_y, HALO), :] = high[k, p] * keep_high

    def place_beside(first, planes, tiles, keep):
        for k, (out, skip) in enumerate(targets):
            for p in range(HALO):
                start = skip + (first + p) * long_y
                out[pl.ds(start, HALO), :] = tiles[k, p] * (keep * keep_low)
                out[pl.ds(start + HALO, size_y), :] = planes[k, p] * keep
                out[pl.ds(start + HALO + size_y, HALO), :] = tiles[k, HALO - 1 - p] * (
                    keep * keep_high
                )

    odd_n = is_odd("narrow")
    for flag_n in (False, True):
        for flag_w in (False, True):

            @pl.when(jnp.logical_and(odd_n == flag_n, odd_w == flag_w))
            def _(flag_n=flag_n, flag_w=flag_w):
                rows = (rows_inner, rows_outer) if flag_n else (rows_outer, rows_inner)
                place_own(*rows, *((near, far) if flag_w else (far, near)))

    @pl.when(odd_w)
    def _():
        place_beside(0, planes_inner, corner_inner, keep_left)
        place_beside(HALO + size_x, planes_outer, corner_outer, keep_right)

    @pl.when(jnp.logical_not(odd_w))
    def _():
        place_beside(0, planes_outer, corner_outer, keep_left)
        place_beside(HALO + size_x, planes_inner, corner_inner, keep_right)

    empty = jnp.zeros((long_y, size_z), jnp.float32)
    cond[at(0), :] = empty
    cond[at(long_x + 1), :] = empty

    lane = lax.broadcasted_iota(jnp.int32, (long_y, size_z), 1)
    row = lax.broadcasted_iota(jnp.int32, (long_y, size_z), 0)
    unit = 1.0 / spread_scale
    half = 0.5 * unit
    mask_y = jnp.where(row == HALO, keep_low, jnp.where(row == HALO + size_y, keep_high, 1.0))
    mask_yp = jnp.where(
        row == HALO - 1, keep_low, jnp.where(row == HALO + size_y - 1, keep_high, 1.0)
    )

    def turn(value):
        return (
            jnp.where(lane == 0, 0.0, pltpu.roll(value, 1, 1)),
            jnp.where(lane == size_z - 1, 0.0, pltpu.roll(value, size_z - 1, 1)),
        )

    def turn_start(x):
        here = field[at(x), :]
        back_a[at(x), :] = pltpu.roll(here, 1, 1)
        front_a[at(x), :] = pltpu.roll(here, size_z - 1, 1)
        back, front = turn(cond[at(x + 1), :])
        back_b[at(x), :] = back
        front_b[at(x), :] = front

    def coefficients(x):
        here = cond[at(x + 1), :]
        left = half * (here + cond[at(x), :])
        right = half * (here + cond[at(x + 2), :])
        low = half * (here + cond[at(x + 1, long_y, -1), :])
        high = half * (here + cond[at(x + 1, long_y, 1), :])
        z_low = half * (here + back_b[at(x), :])
        z_high = half * (here + front_b[at(x), :])
        face_x[at(x), :] = left
        face_y[at(x), :] = low * mask_y
        face_yp[at(x), :] = high * mask_yp
        face_z[at(x), :] = jnp.where(lane == 0, 0.0, z_low)
        face_zp[at(x), :] = jnp.where(lane == size_z - 1, 0.0, z_high)
        diag[at(x), :] = unit * diag[at(x), :] + ((left + right) + (low + high) + (z_low + z_high))

    group = 4

    def start_group(g, _):
        for i in range(group):
            coefficients((g - 1) * group + i)
        for i in range(group):
            turn_start(g * group + i)
        return 0

    for i in range(group):
        turn_start(i)
    lax.fori_loop(1, long_x // group, start_group, 0)
    for i in range(group):
        coefficients(long_x - group + i)
    face_x[at(HALO), :] = face_x[at(HALO), :] * keep_left
    face_x[at(HALO + size_x), :] = face_x[at(HALO + size_x), :] * keep_right

    def step(number, read, back, front, write, next_back, next_front):
        theta = shifts[number] * unit
        final = number == STEPS - 1
        low, count = (HALO, size_y) if final else (0, long_y)

        def plane(x):
            rows = at(x, count, low)
            here = read[rows, :]
            beside = (
                face_x[at(x + 1, count, low), :] * read[at(x + 1, count, low), :]
                + face_x[rows, :] * read[at(x - 1, count, low), :]
            )
            across = (
                face_yp[rows, :] * read[at(x, count, low + 1), :]
                + face_y[rows, :] * read[at(x, count, low - 1), :]
            )
            along = face_zp[rows, :] * front[rows, :] + face_z[rows, :] * back[rows, :]
            write[rows, :] = (diag[rows, :] - theta) * here - (beside + across + along)

        def turn_plane(x):
            if not final:
                here = write[at(x), :]
                next_back[at(x), :] = pltpu.roll(here, 1, 1)
                next_front[at(x), :] = pltpu.roll(here, size_z - 1, 1)

        start, stop = number + 1, long_x - 1 - number
        head = (stop - start) % group or group
        for x in range(start, start + head):
            plane(x)
        for x in range(start + 1, start + head):
            turn_plane(x)
        begin = start + head
        for x in range(begin, begin + group):
            plane(x)

        def body(g, _):
            x = begin + g * group
            for i in range(group):
                turn_plane(x - group + i)
            for i in range(group):
                plane(x + i)
            return 0

        lax.fori_loop(1, (stop - begin) // group, body, 0)
        for x in range(stop - group, stop - 1):
            turn_plane(x)

    turned = ((back_a, front_a), (back_b, front_b))
    for number in range(STEPS):
        step(
            number, basis.at[number], *turned[number % 2],
            basis.at[number + 1], *turned[(number + 1) % 2],
        )

    def own(x):
        return at(x + HALO, size_y, HALO)

    def fold(product):
        parts = [product[8 * t : 8 * t + 8] for t in range(size_y // 8)]
        while len(parts) > 1:
            parts = [a + b for a, b in zip(parts[::2], parts[1::2])]
        return parts[0]

    zero = jnp.zeros((8, size_z), jnp.float32)

    def first_dots(x, sums):
        columns = [basis[j, own(x), :] for j in range(COLS)]
        return tuple(s + fold(columns[0] * c) for s, c in zip(sums, columns))

    sums = lax.fori_loop(0, size_x, first_dots, (zero,) * COLS)
    dots = [total(s) for s in sums]
    index = lax.broadcasted_iota(jnp.int32, (1, 128), 1)
    packed = jnp.zeros((1, 128), jnp.float32)
    for k in range(COLS):
        length = jnp.sqrt(dots[0])
        inverse = jnp.where(dots[0] > 0.0, 1.0 / length, 0.0)
        ratio = [d * inverse * inverse for d in dots]
        for j in range(k, COLS):
            entry = length if j == k else dots[j - k] * inverse
            packed = jnp.where(index == 8 * j + k, entry, packed)
        if k == COLS - 1:
            break

        def sweep(x, sums, k=k, ratio=ratio):
            pivot = field[own(x), :] if k == 0 else work[k, x]
            columns = []
            for j in range(k + 1, COLS):
                old = basis[j, own(x), :] if k == 0 else work[j, x]
                new = old - ratio[j - k] * pivot
                work[j, x] = new
                columns.append(new)
            return tuple(s + fold(columns[0] * c) for s, c in zip(sums, columns))

        sums = lax.fori_loop(0, size_x, sweep, (zero,) * (COLS - 1 - k))
        dots = [total(s) for s in sums]
    rows_out[...] = jnp.broadcast_to(packed, rows_out.shape)


def basis_and_factor(*parts):
    _, half, size_y, size_z = parts[0].shape
    size_x = 2 * half
    long_x, long_y = size_x + 2 * HALO, size_y + 2 * HALO
    devices = lax.axis_size("wide") * lax.axis_size("narrow")
    last = (lax.axis_size("wide") - 1, lax.axis_size("narrow") - 1)
    planes = lambda count: pltpu.VMEM((count * long_y, size_z), jnp.float32)
    return pl.pallas_call(
        lambda *refs: basis_kernel(last, long_y, *refs),
        out_shape=(
            jax.ShapeDtypeStruct((COLS, long_x * long_y, size_z), jnp.float32),
            jax.ShapeDtypeStruct((devices, 128), jnp.float32),
        ),
        in_specs=vmem_spec(8),
        out_specs=tuple(vmem_spec(2)),
        scratch_shapes=[planes(long_x + 2)] + [planes(long_x)] * 10
        + [pltpu.VMEM((COLS, size_x, size_y, size_z), jnp.float32)],
        compiler_params=pltpu.CompilerParams(vmem_limit_bytes=28 * MIB),
        name="basis_and_factor",
    )(*parts)


def split(x):
    big = x * 4097.0
    high = big - (big - x)
    return high, x - high


def two_sum(a, b):
    s = a + b
    t = s - a
    return s, (a - (s - t)) + (b - t)


def small_solve(factor):
    shifts = newton_shifts()
    null = [1.0]
    for theta in shifts:
        null.append(-theta / spread_scale * null[-1])
    inverse = [1.0 / factor[(i, i)] for i in range(COLS)]

    left = [jnp.full((1, 1), w, jnp.float32) for w in null]
    normal = []
    for i in range(COLS):
        normal.append(left[i] * inverse[i])
        for j in range(i + 1, COLS):
            left[j] = left[j] - factor[(i, j)] * normal[i]
    square = normal[0] * normal[0]
    for i in range(1, COLS):
        square = square + normal[i] * normal[i]
    target = [entry / square for entry in normal]

    def back(right):
        right, solved = list(right), [None] * COLS
        for j in range(COLS - 1, -1, -1):
            solved[j] = right[j] * inverse[j]
            for i in range(j):
                right[i] = right[i] - factor[(i, j)] * solved[j]
        return solved

    z = back(target)
    z_parts = [split(entry) for entry in z]
    missing = []
    for i in range(COLS):
        high, low = target[i], None
        for j in range(i, COLS):
            (ah, al), (bh, bl) = split(factor[(i, j)]), z_parts[j]
            product = factor[(i, j)] * z[j]
            error = ((ah * bh - product) + ah * bl + al * bh) + al * bl
            high, carry = two_sum(high, -product)
            carry = carry - error
            low = carry if low is None else low + carry
        missing.append(high + low)
    z = [a + b for a, b in zip(z, back(missing))]

    y = [None] * STEPS
    for j in range(STEPS, 0, -1):
        right = -z[j]
        if j < STEPS:
            right = right - shifts[j] * y[j]
        y[j - 1] = right * (1.0 / spread_scale)
    return y, 1.0 / jnp.sqrt(square), z


def combine_kernel(basis, rows, correction, remainder, upper, norm):
    stacked = rows[...].T
    tops = [stacked[8 * j : 8 * j + 8] for j in range(COLS)]
    tail = stacked[8 * COLS : 8 * COLS + 8]
    sublane = lax.broadcasted_iota(jnp.int32, (8, 128), 0)
    tail = jnp.where(sublane == 0, tail, 0.0)
    factor = {}
    for k in range(COLS):
        square = tops[k] * tops[k]
        if k == COLS - 1:
            square = square + tail * tail
        dots = [total(square)] + [total(tops[k] * tops[j]) for j in range(k + 1, COLS)]
        ridge = dots[0] + 1e-12
        length = jnp.sqrt(ridge)
        again = 2.0 - dots[0] / ridge
        factor[(k, k)] = length
        for j in range(k + 1, COLS):
            factor[(k, j)] = dots[j - k] / length * again
            tops[j] = tops[j] - (dots[j - k] / ridge * again) * tops[k]

    y, size, z = small_solve(factor)

    line = lax.broadcasted_iota(jnp.int32, (16, 128), 0)
    lane = lax.broadcasted_iota(jnp.int32, (16, 128), 1)
    table = jnp.zeros((16, 128), jnp.float32)
    for (i, j), entry in factor.items():
        table = jnp.where(jnp.logical_and(line == i, lane == j), entry, table)
    upper[...] = table[:COLS, :COLS]
    norm[...] = size

    size_x, size_y, _ = correction.shape
    long_y = size_y + 2 * HALO

    def combine(x, _):
        rows = pl.ds(pl.multiple_of((x + HALO) * long_y + HALO, 8), size_y)
        here = basis[0, rows, :]
        first, second = y[0] * here, z[0] * here
        for j in range(1, COLS):
            here = basis[j, rows, :]
            if j < STEPS:
                first = first + y[j] * here
            second = second + z[j] * here
        correction[x] = first
        remainder[x] = second
        return 0

    lax.fori_loop(0, size_x, combine, 0)


def combine(shape, basis, rows):
    block = jax.ShapeDtypeStruct(shape, jnp.float32)
    return pl.pallas_call(
        combine_kernel,
        out_shape=(
            block,
            block,
            jax.ShapeDtypeStruct((COLS, COLS), jnp.float32),
            jax.ShapeDtypeStruct((1, 1), jnp.float32),
        ),
        in_specs=vmem_spec(2),
        out_specs=tuple(vmem_spec(4)),
        compiler_params=pltpu.CompilerParams(vmem_limit_bytes=8 * MIB),
        name="combine",
    )(basis, rows)


def on_device(source, conduct, storage):
    inner, outer, near, far = edges(source, conduct, storage)
    rows = exchange(inner, outer, "narrow")
    planes = exchange(near, far, "wide")
    tiles = exchange(*corners(*rows), "wide")
    basis, packed = basis_and_factor(near, far, *rows, *planes, *tiles)
    gathered = lax.all_to_all(packed, ("wide", "narrow"), 0, 0, tiled=True)
    correction, remainder, factor, resid = combine(source.shape, basis, gathered)
    return correction, remainder, factor, resid[0, 0]


def solution(mesh):
    spec = P("wide", "narrow", None)
    return jax.shard_map(
        on_device,
        mesh=mesh,
        in_specs=(spec, spec, spec),
        out_specs=(spec, spec, P(), P()),
        check_vma=False,
    )
```

```python
import math

import jax
import jax.numpy as jnp
from jax import lax
from jax.experimental import pallas as pl
from jax.experimental.pallas import tpu as pltpu
from jax.sharding import PartitionSpec as P

STEPS = 8
COLS = 9
HALO = 8

leja_order = (0, 7, 3, 5, 2, 6, 1, 4)
spread_scale = 6.5
MIB = 1024 * 1024


def newton_shifts():
    return [
        13.125 + 12.875 * math.cos(math.pi * (2 * position + 1) / 16.0) for position in leja_order
    ]


def is_odd(axis):
    return lax.rem(lax.axis_index(axis), 2) == 1


def exchange(first, second, axis):
    size = lax.axis_size(axis)
    inner = [(i, i ^ 1) for i in range(size)]
    outer = [(i, (((i + 1) % size ^ 1) - 1) % size) for i in range(size)]
    return lax.ppermute(first, axis, inner), lax.ppermute(second, axis, outer)


def vmem_spec(count):
    return [pl.BlockSpec(memory_space=pltpu.VMEM)] * count


def edge_kernel(source, conduct, storage, inner, outer, near, far, sems):
    odd_n, odd_w = is_odd("narrow"), is_odd("wide")
    size_x, width, _ = source.shape
    half = size_x // 2

    def copies(low, high, first, second):
        result = []
        for k, ref in enumerate((source, conduct, storage)):
            result += [
                pltpu.make_async_copy(ref.at[:, pl.ds(0, HALO), :], low.at[k], sems.at[k]),
                pltpu.make_async_copy(
                    ref.at[:, pl.ds(width - HALO, HALO), :], high.at[k], sems.at[3 + k]
                ),
                pltpu.make_async_copy(ref.at[pl.ds(0, half)], first.at[k], sems.at[6 + k]),
                pltpu.make_async_copy(ref.at[pl.ds(half, half)], second.at[k], sems.at[9 + k]),
            ]
        return result

    for flag_n in (False, True):
        for flag_w in (False, True):

            @pl.when(jnp.logical_and(odd_n == flag_n, odd_w == flag_w))
            def _(flag_n=flag_n, flag_w=flag_w):
                rows = (inner, outer) if flag_n else (outer, inner)
                halves = (near, far) if flag_w else (far, near)
                every = copies(*rows, *halves)
                for copy in every:
                    copy.start()
                for copy in every:
                    copy.wait()


def edges(source, conduct, storage):
    size_x, width, size_z = source.shape
    rows = jax.ShapeDtypeStruct((3, size_x, HALO, size_z), jnp.float32)
    halves = jax.ShapeDtypeStruct((3, size_x // 2, width, size_z), jnp.float32)
    return pl.pallas_call(
        edge_kernel,
        out_shape=(rows, rows, halves, halves),
        in_specs=[pl.BlockSpec(memory_space=pltpu.HBM)] * 3,
        out_specs=tuple(vmem_spec(4)),
        scratch_shapes=[pltpu.SemaphoreType.DMA((12,))],
        compiler_params=pltpu.CompilerParams(vmem_limit_bytes=8 * MIB),
        name="edges",
    )(*(pltpu.with_memory_space_constraint(x, pltpu.HBM) for x in (source, conduct, storage)))


def corner_kernel(inner, outer, near, far):
    odd_n, odd_w = is_odd("narrow"), is_odd("wide")
    half = near.shape[1]
    row = lax.broadcasted_iota(jnp.int32, near.shape[2:], 0)

    def fill(low_rows, high_rows, low_half, high_half):
        for k in range(3):
            for p in range(half):
                low_half[k, p] = jnp.where(
                    row >= p + 1, low_rows[k, p], high_rows[k, half - 1 - p]
                )
                high_half[k, p] = jnp.where(
                    row >= half - p, low_rows[k, half + p], high_rows[k, 2 * half - 1 - p]
                )

    for flag_n in (False, True):
        for flag_w in (False, True):

            @pl.when(jnp.logical_and(odd_n == flag_n, odd_w == flag_w))
            def _(flag_n=flag_n, flag_w=flag_w):
                rows = (inner, outer) if flag_n else (outer, inner)
                halves = (near, far) if flag_w else (far, near)
                fill(*rows, *halves)


def corners(inner, outer):
    _, size_x, rows, size_z = inner.shape
    shape = jax.ShapeDtypeStruct((3, size_x // 2, rows, size_z), jnp.float32)
    return pl.pallas_call(
        corner_kernel,
        out_shape=(shape, shape),
        in_specs=vmem_spec(2),
        out_specs=tuple(vmem_spec(2)),
        compiler_params=pltpu.CompilerParams(vmem_limit_bytes=8 * MIB),
        name="corners",
    )(inner, outer)


def total(x):
    return jnp.sum(jnp.sum(x, axis=0, keepdims=True), axis=1, keepdims=True)


def basis_kernel(
    last, long_y, near, far, rows_inner, rows_outer, planes_inner, planes_outer,
    corner_inner, corner_outer, basis, rows_out,
    cond, diag, face_x, face_y, face_yp, face_z, face_zp,
    back_a, front_a, back_b, front_b, work,
):
    odd_w = is_odd("wide")
    place_w, place_n = lax.axis_index("wide"), lax.axis_index("narrow")
    keep_left = jnp.where(place_w == 0, 0.0, 1.0)
    keep_right = jnp.where(place_w == last[0], 0.0, 1.0)
    keep_low = jnp.where(place_n == 0, 0.0, 1.0)
    keep_high = jnp.where(place_n == last[1], 0.0, 1.0)
    field = basis.at[0]
    size_z = diag.shape[1]
    long_x = diag.shape[0] // long_y
    size_x, size_y = long_x - 2 * HALO, long_y - 2 * HALO
    shifts = newton_shifts()

    def at(x, count=long_y, first=0):
        start = x * long_y + first
        if not isinstance(x, int) and first % 8 == 0:
            start = pl.multiple_of(start, 8)
        return pl.ds(start, count)

    targets = ((field, 0), (cond, long_y), (diag, 0))

    def place_own(low, high, first, second):
        half = size_x // 2
        for k, (out, skip) in enumerate(targets):
            for p in range(size_x):
                start = skip + (HALO + p) * long_y
                out[pl.ds(start, HALO), :] = low[k, p] * keep_low
                own = first[k, p] if p < half else second[k, p - half]
                out[pl.ds(start + HALO, size_y), :] = own
                out[pl.ds(start + HALO + size_y, HALO), :] = high[k, p] * keep_high

    def place_beside(first, planes, tiles, keep):
        for k, (out, skip) in enumerate(targets):
            for p in range(HALO):
                start = skip + (first + p) * long_y
                out[pl.ds(start, HALO), :] = tiles[k, p] * (keep * keep_low)
                out[pl.ds(start + HALO, size_y), :] = planes[k, p] * keep
                out[pl.ds(start + HALO + size_y, HALO), :] = tiles[k, HALO - 1 - p] * (
                    keep * keep_high
                )

    odd_n = is_odd("narrow")
    for flag_n in (False, True):
        for flag_w in (False, True):

            @pl.when(jnp.logical_and(odd_n == flag_n, odd_w == flag_w))
            def _(flag_n=flag_n, flag_w=flag_w):
                rows = (rows_inner, rows_outer) if flag_n else (rows_outer, rows_inner)
                place_own(*rows, *((near, far) if flag_w else (far, near)))

    @pl.when(odd_w)
    def _():
        place_beside(0, planes_inner, corner_inner, keep_left)
        place_beside(HALO + size_x, planes_outer, corner_outer, keep_right)

    @pl.when(jnp.logical_not(odd_w))
    def _():
        place_beside(0, planes_outer, corner_outer, keep_left)
        place_beside(HALO + size_x, planes_inner, corner_inner, keep_right)

    empty = jnp.zeros((long_y, size_z), jnp.float32)
    cond[at(0), :] = empty
    cond[at(long_x + 1), :] = empty

    lane = lax.broadcasted_iota(jnp.int32, (long_y, size_z), 1)
    row = lax.broadcasted_iota(jnp.int32, (long_y, size_z), 0)
    unit = 1.0 / spread_scale
    half = 0.5 * unit
    mask_y = jnp.where(row == HALO, keep_low, jnp.where(row == HALO + size_y, keep_high, 1.0))
    mask_yp = jnp.where(
        row == HALO - 1, keep_low, jnp.where(row == HALO + size_y - 1, keep_high, 1.0)
    )

    def turn(value):
        return (
            jnp.where(lane == 0, 0.0, pltpu.roll(value, 1, 1)),
            jnp.where(lane == size_z - 1, 0.0, pltpu.roll(value, size_z - 1, 1)),
        )

    def turn_start(x):
        here = field[at(x), :]
        back_a[at(x), :] = pltpu.roll(here, 1, 1)
        front_a[at(x), :] = pltpu.roll(here, size_z - 1, 1)
        back, front = turn(cond[at(x + 1), :])
        back_b[at(x), :] = back
        front_b[at(x), :] = front

    def coefficients(x):
        here = cond[at(x + 1), :]
        left = half * (here + cond[at(x), :])
        right = half * (here + cond[at(x + 2), :])
        low = half * (here + cond[at(x + 1, long_y, -1), :])
        high = half * (here + cond[at(x + 1, long_y, 1), :])
        z_low = half * (here + back_b[at(x), :])
        z_high = half * (here + front_b[at(x), :])
        face_x[at(x), :] = left
        face_y[at(x), :] = low * mask_y
        face_yp[at(x), :] = high * mask_yp
        face_z[at(x), :] = jnp.where(lane == 0, 0.0, z_low)
        face_zp[at(x), :] = jnp.where(lane == size_z - 1, 0.0, z_high)
        diag[at(x), :] = unit * diag[at(x), :] + ((left + right) + (low + high) + (z_low + z_high))

    group = 16

    def start_group(g, _):
        for i in range(group):
            coefficients((g - 1) * group + i)
        for i in range(group):
            turn_start(g * group + i)
        return 0

    for i in range(group):
        turn_start(i)
    lax.fori_loop(1, long_x // group, start_group, 0)
    for i in range(group):
        coefficients(long_x - group + i)
    face_x[at(HALO), :] = face_x[at(HALO), :] * keep_left
    face_x[at(HALO + size_x), :] = face_x[at(HALO + size_x), :] * keep_right

    group = 12

    def step(number, read, back, front, write, next_back, next_front):
        theta = shifts[number] * unit
        final = number == STEPS - 1
        low, count = (HALO, size_y) if final else (0, long_y)

        def plane(x):
            rows = at(x, count, low)
            here = read[rows, :]
            beside = (
                face_x[at(x + 1, count, low), :] * read[at(x + 1, count, low), :]
                + face_x[rows, :] * read[at(x - 1, count, low), :]
            )
            across = (
                face_yp[rows, :] * read[at(x, count, low + 1), :]
                + face_y[rows, :] * read[at(x, count, low - 1), :]
            )
            along = face_zp[rows, :] * front[rows, :] + face_z[rows, :] * back[rows, :]
            write[rows, :] = (diag[rows, :] - theta) * here - (beside + across + along)

        def turn_plane(x):
            if not final:
                here = write[at(x), :]
                next_back[at(x), :] = pltpu.roll(here, 1, 1)
                next_front[at(x), :] = pltpu.roll(here, size_z - 1, 1)

        start, stop = number + 1, long_x - 1 - number
        head = (stop - start) % group or group
        for x in range(start, start + head):
            plane(x)
        for x in range(start + 1, start + head):
            turn_plane(x)
        begin = start + head
        for x in range(begin, begin + group):
            plane(x)

        def body(g, _):
            x = begin + g * group
            for i in range(group):
                turn_plane(x - group + i)
            for i in range(group):
                plane(x + i)
            return 0

        lax.fori_loop(1, (stop - begin) // group, body, 0)
        for x in range(stop - group, stop - 1):
            turn_plane(x)

    turned = ((back_a, front_a), (back_b, front_b))
    for number in range(STEPS):
        step(
            number, basis.at[number], *turned[number % 2],
            basis.at[number + 1], *turned[(number + 1) % 2],
        )

    def own(x):
        return at(x + HALO, size_y, HALO)

    def fold(product):
        parts = [product[8 * t : 8 * t + 8] for t in range(size_y // 8)]
        while len(parts) > 1:
            parts = [a + b for a, b in zip(parts[::2], parts[1::2])]
        return parts[0]

    zero = jnp.zeros((8, size_z), jnp.float32)

    def first_dots(x, sums):
        columns = [basis[j, own(x), :] for j in range(COLS)]
        return tuple(s + fold(columns[0] * c) for s, c in zip(sums, columns))

    sums = lax.fori_loop(0, size_x, first_dots, (zero,) * COLS, unroll=True)
    dots = [total(s) for s in sums]
    index = lax.broadcasted_iota(jnp.int32, (1, 128), 1)
    packed = jnp.zeros((1, 128), jnp.float32)
    for k in range(COLS):
        length = jnp.sqrt(dots[0])
        inverse = jnp.where(dots[0] > 0.0, 1.0 / length, 0.0)
        ratio = [d * inverse * inverse for d in dots]
        for j in range(k, COLS):
            entry = length if j == k else dots[j - k] * inverse
            packed = jnp.where(index == 8 * j + k, entry, packed)
        if k == COLS - 1:
            break

        def sweep(x, sums, k=k, ratio=ratio):
            pivot = field[own(x), :] if k == 0 else work[k, x]
            columns = []
            for j in range(k + 1, COLS):
                old = basis[j, own(x), :] if k == 0 else work[j, x]
                new = old - ratio[j - k] * pivot
                work[j, x] = new
                columns.append(new)
            return tuple(s + fold(columns[0] * c) for s, c in zip(sums, columns))

        sums = lax.fori_loop(
            0, size_x, sweep, (zero,) * (COLS - 1 - k), unroll=True
        )
        dots = [total(s) for s in sums]
    rows_out[...] = jnp.broadcast_to(packed, rows_out.shape)


def basis_and_factor(*parts):
    _, half, size_y, size_z = parts[0].shape
    size_x = 2 * half
    long_x, long_y = size_x + 2 * HALO, size_y + 2 * HALO
    devices = lax.axis_size("wide") * lax.axis_size("narrow")
    last = (lax.axis_size("wide") - 1, lax.axis_size("narrow") - 1)
    planes = lambda count: pltpu.VMEM((count * long_y, size_z), jnp.float32)
    return pl.pallas_call(
        lambda *refs: basis_kernel(last, long_y, *refs),
        out_shape=(
            jax.ShapeDtypeStruct((COLS, long_x * long_y, size_z), jnp.float32),
            jax.ShapeDtypeStruct((devices, 128), jnp.float32),
        ),
        in_specs=vmem_spec(8),
        out_specs=tuple(vmem_spec(2)),
        scratch_shapes=[planes(long_x + 2)] + [planes(long_x)] * 10
        + [pltpu.VMEM((COLS, size_x, size_y, size_z), jnp.float32)],
        compiler_params=pltpu.CompilerParams(vmem_limit_bytes=28 * MIB),
        name="basis_and_factor",
    )(*parts)


def split(x):
    big = x * 4097.0
    high = big - (big - x)
    return high, x - high


def two_sum(a, b):
    s = a + b
    t = s - a
    return s, (a - (s - t)) + (b - t)


def small_solve(factor):
    shifts = newton_shifts()
    null = [1.0]
    for theta in shifts:
        null.append(-theta / spread_scale * null[-1])
    inverse = [1.0 / factor[(i, i)] for i in range(COLS)]

    left = [jnp.full((1, 1), w, jnp.float32) for w in null]
    normal = []
    for i in range(COLS):
        normal.append(left[i] * inverse[i])
        for j in range(i + 1, COLS):
            left[j] = left[j] - factor[(i, j)] * normal[i]
    square = normal[0] * normal[0]
    for i in range(1, COLS):
        square = square + normal[i] * normal[i]
    target = [entry / square for entry in normal]

    def back(right):
        right, solved = list(right), [None] * COLS
        for j in range(COLS - 1, -1, -1):
            solved[j] = right[j] * inverse[j]
            for i in range(j):
                right[i] = right[i] - factor[(i, j)] * solved[j]
        return solved

    z = back(target)
    z_parts = [split(entry) for entry in z]
    missing = []
    for i in range(COLS):
        high, low = target[i], None
        for j in range(i, COLS):
            (ah, al), (bh, bl) = split(factor[(i, j)]), z_parts[j]
            product = factor[(i, j)] * z[j]
            error = ((ah * bh - product) + ah * bl + al * bh) + al * bl
            high, carry = two_sum(high, -product)
            carry = carry - error
            low = carry if low is None else low + carry
        missing.append(high + low)
    z = [a + b for a, b in zip(z, back(missing))]

    y = [None] * STEPS
    for j in range(STEPS, 0, -1):
        right = -z[j]
        if j < STEPS:
            right = right - shifts[j] * y[j]
        y[j - 1] = right * (1.0 / spread_scale)
    return y, 1.0 / jnp.sqrt(square), z


def combine_kernel(basis, rows, correction, remainder, upper, norm):
    stacked = rows[...].T
    tops = [stacked[8 * j : 8 * j + 8] for j in range(COLS)]
    tail = stacked[8 * COLS : 8 * COLS + 8]
    sublane = lax.broadcasted_iota(jnp.int32, (8, 128), 0)
    tail = jnp.where(sublane == 0, tail, 0.0)
    factor = {}
    for k in range(COLS):
        square = tops[k] * tops[k]
        if k == COLS - 1:
            square = square + tail * tail
        dots = [total(square)] + [total(tops[k] * tops[j]) for j in range(k + 1, COLS)]
        ridge = dots[0] + 1e-12
        length = jnp.sqrt(ridge)
        again = 2.0 - dots[0] / ridge
        factor[(k, k)] = length
        for j in range(k + 1, COLS):
            factor[(k, j)] = dots[j - k] / length * again
            tops[j] = tops[j] - (dots[j - k] / ridge * again) * tops[k]

    y, size, z = small_solve(factor)

    line = lax.broadcasted_iota(jnp.int32, (16, 128), 0)
    lane = lax.broadcasted_iota(jnp.int32, (16, 128), 1)
    table = jnp.zeros((16, 128), jnp.float32)
    for (i, j), entry in factor.items():
        table = jnp.where(jnp.logical_and(line == i, lane == j), entry, table)
    upper[...] = table[:COLS, :COLS]
    norm[...] = size

    size_x, size_y, _ = correction.shape
    long_y = size_y + 2 * HALO

    def combine(x, _):
        rows = pl.ds(pl.multiple_of((x + HALO) * long_y + HALO, 8), size_y)
        here = basis[0, rows, :]
        first, second = y[0] * here, z[0] * here
        for j in range(1, COLS):
            here = basis[j, rows, :]
            if j < STEPS:
                first = first + y[j] * here
            second = second + z[j] * here
        correction[x] = first
        remainder[x] = second
        return 0

    lax.fori_loop(0, size_x, combine, 0, unroll=4)


def combine(shape, basis, rows):
    block = jax.ShapeDtypeStruct(shape, jnp.float32)
    return pl.pallas_call(
        combine_kernel,
        out_shape=(
            block,
            block,
            jax.ShapeDtypeStruct((COLS, COLS), jnp.float32),
            jax.ShapeDtypeStruct((1, 1), jnp.float32),
        ),
        in_specs=vmem_spec(2),
        out_specs=tuple(vmem_spec(4)),
        compiler_params=pltpu.CompilerParams(vmem_limit_bytes=8 * MIB),
        name="combine",
    )(basis, rows)


def on_device(source, conduct, storage):
    inner, outer, near, far = edges(source, conduct, storage)
    rows = exchange(inner, outer, "narrow")
    planes = exchange(near, far, "wide")
    tiles = exchange(*corners(*rows), "wide")
    basis, packed = basis_and_factor(near, far, *rows, *planes, *tiles)
    gathered = lax.all_to_all(packed, ("wide", "narrow"), 0, 0, tiled=True)
    correction, remainder, factor, resid = combine(source.shape, basis, gathered)
    return correction, remainder, factor, resid[0, 0]


def solution(mesh):
    spec = P("wide", "narrow", None)
    return jax.shard_map(
        on_device,
        mesh=mesh,
        in_specs=(spec, spec, spec),
        out_specs=(spec, spec, P(), P()),
        check_vma=False,
    )
```

```python
import math

import jax
import jax.numpy as jnp
from jax import lax
from jax.experimental import pallas as pl
from jax.experimental.pallas import tpu as pltpu
from jax.sharding import PartitionSpec as P

STEPS = 8
COLS = 9
HALO = 8

leja_order = (0, 7, 3, 5, 2, 6, 1, 4)
spread_scale = 6.5
MIB = 1024 * 1024


def newton_shifts():
    return [
        13.125 + 12.875 * math.cos(math.pi * (2 * position + 1) / 16.0) for position in leja_order
    ]


def is_odd(axis):
    return lax.rem(lax.axis_index(axis), 2) == 1


def swap(block, axis, shift):
    axes = ("wide", "narrow")
    sizes = [lax.axis_size(name) for name in axes]
    along = axes.index(axis)
    pairs = []
    for i in range(sizes[0]):
        for j in range(sizes[1]):
            to = [i, j]
            to[along] = (to[along] + shift ^ 1) - shift
            if not 0 <= to[along] < sizes[along]:
                to = [i, j]
                to[1 - along] ^= 1
            pairs.append((i * sizes[1] + j, to[0] * sizes[1] + to[1]))
    return lax.ppermute(block, axes, pairs)


def exchange(inner, outer, axis):
    return swap(inner, axis, 0), swap(outer, axis, 1)


def vmem_spec(count):
    return [pl.BlockSpec(memory_space=pltpu.VMEM)] * count


def edge_kernel(source, conduct, storage, inner, outer, near, far, sems):
    odd_n, odd_w = is_odd("narrow"), is_odd("wide")
    size_x, width, _ = source.shape
    half = size_x // 2

    def copies(low, high, first, second):
        result = []
        for k, ref in enumerate((source, conduct, storage)):
            result += [
                pltpu.make_async_copy(ref.at[:, pl.ds(0, HALO), :], low.at[k], sems.at[k]),
                pltpu.make_async_copy(
                    ref.at[:, pl.ds(width - HALO, HALO), :], high.at[k], sems.at[3 + k]
                ),
                pltpu.make_async_copy(ref.at[pl.ds(0, half)], first.at[k], sems.at[6 + k]),
                pltpu.make_async_copy(ref.at[pl.ds(half, half)], second.at[k], sems.at[9 + k]),
            ]
        return result

    for flag_n in (False, True):
        for flag_w in (False, True):

            @pl.when(jnp.logical_and(odd_n == flag_n, odd_w == flag_w))
            def _(flag_n=flag_n, flag_w=flag_w):
                rows = (inner, outer) if flag_n else (outer, inner)
                halves = (near, far) if flag_w else (far, near)
                every = copies(*rows, *halves)
                for copy in every:
                    copy.start()
                for copy in every:
                    copy.wait()


def edges(source, conduct, storage):
    size_x, width, size_z = source.shape
    rows = jax.ShapeDtypeStruct((3, size_x, HALO, size_z), jnp.float32)
    halves = jax.ShapeDtypeStruct((3, size_x // 2, width, size_z), jnp.float32)
    return pl.pallas_call(
        edge_kernel,
        out_shape=(rows, rows, halves, halves),
        in_specs=[pl.BlockSpec(memory_space=pltpu.HBM)] * 3,
        out_specs=tuple(vmem_spec(4)),
        scratch_shapes=[pltpu.SemaphoreType.DMA((12,))],
        compiler_params=pltpu.CompilerParams(vmem_limit_bytes=8 * MIB),
        name="edges",
    )(*(pltpu.with_memory_space_constraint(x, pltpu.HBM) for x in (source, conduct, storage)))


def corner_kernel(inner, outer, own, _, near, far):
    odd_n, odd_w = is_odd("narrow"), is_odd("wide")
    half = near.shape[1]
    row = lax.broadcasted_iota(jnp.int32, far.shape[2:], 0)
    for k in range(3):
        for p in range(half):
            near[k, p, HALO:, :] = own[k, p]

    def fill(low_rows, high_rows, low_half, high_half):
        for k in range(3):
            for p in range(half):
                low_half[k, p, 0:HALO, :] = jnp.where(
                    row >= p + 1, low_rows[k, p], high_rows[k, half - 1 - p]
                )
                high_half[k, p, 0:HALO, :] = jnp.where(
                    row >= half - p, low_rows[k, half + p], high_rows[k, 2 * half - 1 - p]
                )

    for flag_n in (False, True):
        for flag_w in (False, True):

            @pl.when(jnp.logical_and(odd_n == flag_n, odd_w == flag_w))
            def _(flag_n=flag_n, flag_w=flag_w):
                rows = (inner, outer) if flag_n else (outer, inner)
                halves = (near, far) if flag_w else (far, near)
                fill(*rows, *halves)


def corners(inner, outer, own, wait):
    _, size_x, rows, size_z = inner.shape
    shape = lambda count: jax.ShapeDtypeStruct((3, size_x // 2, count, size_z), jnp.float32)
    return pl.pallas_call(
        corner_kernel,
        out_shape=(shape(rows + own.shape[2]), shape(rows)),
        in_specs=vmem_spec(4),
        out_specs=tuple(vmem_spec(2)),
        compiler_params=pltpu.CompilerParams(vmem_limit_bytes=8 * MIB),
        name="corners",
    )(inner, outer, own, wait)


def total(x):
    return jnp.sum(jnp.sum(x, axis=0, keepdims=True), axis=1, keepdims=True)


def basis_kernel(
    last, long_y, near, far, rows_inner, rows_outer, planes_inner, planes_outer,
    corner_outer, basis, rows_out,
    cond, diag, face_x, face_y, face_yp, face_z, face_zp,
    back_a, front_a, back_b, front_b, work,
):
    odd_w = is_odd("wide")
    place_w, place_n = lax.axis_index("wide"), lax.axis_index("narrow")
    keep_left = jnp.where(place_w == 0, 0.0, 1.0)
    keep_right = jnp.where(place_w == last[0], 0.0, 1.0)
    keep_low = jnp.where(place_n == 0, 0.0, 1.0)
    keep_high = jnp.where(place_n == last[1], 0.0, 1.0)
    field = basis.at[0]
    size_z = diag.shape[1]
    long_x = diag.shape[0] // long_y
    size_x, size_y = long_x - 2 * HALO, long_y - 2 * HALO
    shifts = newton_shifts()

    def at(x, count=long_y, first=0):
        start = x * long_y + first
        if not isinstance(x, int) and first % 8 == 0:
            start = pl.multiple_of(start, 8)
        return pl.ds(start, count)

    targets = ((field, 0), (cond, long_y), (diag, 0))

    def place_own(low, high, first, second):
        half = size_x // 2
        for k, (out, skip) in enumerate(targets):
            for p in range(size_x):
                start = skip + (HALO + p) * long_y
                out[pl.ds(start, HALO), :] = low[k, p] * keep_low
                own = first[k, p] if p < half else second[k, p - half]
                out[pl.ds(start + HALO, size_y), :] = own
                out[pl.ds(start + HALO + size_y, HALO), :] = high[k, p] * keep_high

    def place_beside(first, planes, tiles, keep):
        for k, (out, skip) in enumerate(targets):
            for p in range(HALO):
                start = skip + (first + p) * long_y
                own = planes[k, p, planes.shape[2] - size_y :, :]
                out[pl.ds(start, HALO), :] = tiles[k, p, 0:HALO, :] * (keep * keep_low)
                out[pl.ds(start + HALO, size_y), :] = own * keep
                out[pl.ds(start + HALO + size_y, HALO), :] = tiles[
                    k, HALO - 1 - p, 0:HALO, :
                ] * (keep * keep_high)

    odd_n = is_odd("narrow")
    for flag_n in (False, True):
        for flag_w in (False, True):

            @pl.when(jnp.logical_and(odd_n == flag_n, odd_w == flag_w))
            def _(flag_n=flag_n, flag_w=flag_w):
                rows = (rows_inner, rows_outer) if flag_n else (rows_outer, rows_inner)
                place_own(*rows, *((near, far) if flag_w else (far, near)))

    @pl.when(odd_w)
    def _():
        place_beside(0, planes_inner, planes_inner, keep_left)
        place_beside(HALO + size_x, planes_outer, corner_outer, keep_right)

    @pl.when(jnp.logical_not(odd_w))
    def _():
        place_beside(0, planes_outer, corner_outer, keep_left)
        place_beside(HALO + size_x, planes_inner, planes_inner, keep_right)

    empty = jnp.zeros((long_y, size_z), jnp.float32)
    cond[at(0), :] = empty
    cond[at(long_x + 1), :] = empty

    lane = lax.broadcasted_iota(jnp.int32, (long_y, size_z), 1)
    row = lax.broadcasted_iota(jnp.int32, (long_y, size_z), 0)
    unit = 1.0 / spread_scale
    half = 0.5 * unit
    mask_y = jnp.where(row == HALO, keep_low, jnp.where(row == HALO + size_y, keep_high, 1.0))
    mask_yp = jnp.where(
        row == HALO - 1, keep_low, jnp.where(row == HALO + size_y - 1, keep_high, 1.0)
    )

    def turn(value):
        return (
            jnp.where(lane == 0, 0.0, pltpu.roll(value, 1, 1)),
            jnp.where(lane == size_z - 1, 0.0, pltpu.roll(value, size_z - 1, 1)),
        )

    def turn_start(x):
        here = field[at(x), :]
        back_a[at(x), :] = pltpu.roll(here, 1, 1)
        front_a[at(x), :] = pltpu.roll(here, size_z - 1, 1)
        back, front = turn(cond[at(x + 1), :])
        back_b[at(x), :] = back
        front_b[at(x), :] = front

    def coefficients(x):
        here = cond[at(x + 1), :]
        left = half * (here + cond[at(x), :])
        right = half * (here + cond[at(x + 2), :])
        low = half * (here + cond[at(x + 1, long_y, -1), :])
        high = half * (here + cond[at(x + 1, long_y, 1), :])
        z_low = half * (here + back_b[at(x), :])
        z_high = half * (here + front_b[at(x), :])
        face_x[at(x), :] = left
        face_y[at(x), :] = low * mask_y
        face_yp[at(x), :] = high * mask_yp
        face_z[at(x), :] = jnp.where(lane == 0, 0.0, z_low)
        face_zp[at(x), :] = jnp.where(lane == size_z - 1, 0.0, z_high)
        diag[at(x), :] = unit * diag[at(x), :] + ((left + right) + (low + high) + (z_low + z_high))

    group = 16

    def start_group(g, _):
        for i in range(group):
            coefficients((g - 1) * group + i)
        for i in range(group):
            turn_start(g * group + i)
        return 0

    for i in range(group):
        turn_start(i)
    lax.fori_loop(1, long_x // group, start_group, 0)
    for i in range(group):
        coefficients(long_x - group + i)
    face_x[at(HALO), :] = face_x[at(HALO), :] * keep_left
    face_x[at(HALO + size_x), :] = face_x[at(HALO + size_x), :] * keep_right

    group = 12

    def step(number, read, back, front, write, next_back, next_front):
        theta = shifts[number] * unit
        final = number == STEPS - 1
        low, count = (HALO, size_y) if final else (0, long_y)

        def plane(x):
            rows = at(x, count, low)
            here = read[rows, :]
            beside = (
                face_x[at(x + 1, count, low), :] * read[at(x + 1, count, low), :]
                + face_x[rows, :] * read[at(x - 1, count, low), :]
            )
            across = (
                face_yp[rows, :] * read[at(x, count, low + 1), :]
                + face_y[rows, :] * read[at(x, count, low - 1), :]
            )
            along = face_zp[rows, :] * front[rows, :] + face_z[rows, :] * back[rows, :]
            write[rows, :] = (diag[rows, :] - theta) * here - (beside + across + along)

        def turn_plane(x):
            if not final:
                rows = at(x, size_y, HALO) if number == STEPS - 2 else at(x)
                here = write[rows, :]
                next_back[rows, :] = pltpu.roll(here, 1, 1)
                next_front[rows, :] = pltpu.roll(here, size_z - 1, 1)

        start, stop = number + 1, long_x - 1 - number
        head = (stop - start) % group or group
        for x in range(start, start + head):
            plane(x)
        for x in range(start + 1, start + head):
            turn_plane(x)
        begin = start + head
        for x in range(begin, begin + group):
            plane(x)

        def body(g, _):
            x = begin + g * group
            for i in range(group):
                turn_plane(x - group + i)
            for i in range(group):
                plane(x + i)
            return 0

        lax.fori_loop(1, (stop - begin) // group, body, 0)
        for x in range(stop - group, stop - 1):
            turn_plane(x)

    turned = ((back_a, front_a), (back_b, front_b))
    for number in range(STEPS):
        step(
            number, basis.at[number], *turned[number % 2],
            basis.at[number + 1], *turned[(number + 1) % 2],
        )

    def own(x):
        return at(x + HALO, size_y, HALO)

    def fold(product):
        parts = [product[8 * t : 8 * t + 8] for t in range(size_y // 8)]
        while len(parts) > 1:
            parts = [a + b for a, b in zip(parts[::2], parts[1::2])]
        return parts[0]

    zero = jnp.zeros((8, size_z), jnp.float32)

    def first_dots(x, sums):
        columns = [basis[j, own(x), :] for j in range(COLS)]
        return tuple(s + fold(columns[0] * c) for s, c in zip(sums, columns))

    sums = lax.fori_loop(0, size_x, first_dots, (zero,) * COLS, unroll=True)
    dots = [total(s) for s in sums]
    index = lax.broadcasted_iota(jnp.int32, (1, 128), 1)
    packed = jnp.zeros((1, 128), jnp.float32)
    for k in range(COLS):
        length = jnp.sqrt(dots[0])
        inverse = jnp.where(dots[0] > 0.0, 1.0 / length, 0.0)
        ratio = [d * inverse * inverse for d in dots]
        for j in range(k, COLS):
            entry = length if j == k else dots[j - k] * inverse
            packed = jnp.where(index == 8 * j + k, entry, packed)
        if k == COLS - 1:
            break

        def sweep(x, sums, k=k, ratio=ratio):
            pivot = field[own(x), :] if k == 0 else work[k, x]
            columns = []
            for j in range(k + 1, COLS):
                old = basis[j, own(x), :] if k == 0 else work[j, x]
                new = old - ratio[j - k] * pivot
                work[j, x] = new
                columns.append(new)
            return tuple(s + fold(columns[0] * c) for s, c in zip(sums, columns))

        sums = lax.fori_loop(
            0, size_x, sweep, (zero,) * (COLS - 1 - k), unroll=True
        )
        dots = [total(s) for s in sums]
    rows_out[...] = jnp.broadcast_to(packed, rows_out.shape)


def basis_and_factor(*parts):
    _, half, size_y, size_z = parts[0].shape
    size_x = 2 * half
    long_x, long_y = size_x + 2 * HALO, size_y + 2 * HALO
    devices = lax.axis_size("wide") * lax.axis_size("narrow")
    last = (lax.axis_size("wide") - 1, lax.axis_size("narrow") - 1)
    planes = lambda count: pltpu.VMEM((count * long_y, size_z), jnp.float32)
    return pl.pallas_call(
        lambda *refs: basis_kernel(last, long_y, *refs),
        out_shape=(
            jax.ShapeDtypeStruct((COLS, long_x * long_y, size_z), jnp.float32),
            jax.ShapeDtypeStruct((devices, 128), jnp.float32),
        ),
        in_specs=vmem_spec(7),
        out_specs=tuple(vmem_spec(2)),
        scratch_shapes=[planes(long_x + 2)] + [planes(long_x)] * 10
        + [pltpu.VMEM((COLS, size_x, size_y, size_z), jnp.float32)],
        compiler_params=pltpu.CompilerParams(vmem_limit_bytes=28 * MIB),
        name="basis_and_factor",
    )(*parts)


def split(x):
    big = x * 4097.0
    high = big - (big - x)
    return high, x - high


def two_sum(a, b):
    s = a + b
    t = s - a
    return s, (a - (s - t)) + (b - t)


def small_solve(factor):
    shifts = newton_shifts()
    null = [1.0]
    for theta in shifts:
        null.append(-theta / spread_scale * null[-1])
    inverse = [1.0 / factor[(i, i)] for i in range(COLS)]

    left = [jnp.full((1, 1), w, jnp.float32) for w in null]
    normal = []
    for i in range(COLS):
        normal.append(left[i] * inverse[i])
        for j in range(i + 1, COLS):
            left[j] = left[j] - factor[(i, j)] * normal[i]
    square = normal[0] * normal[0]
    for i in range(1, COLS):
        square = square + normal[i] * normal[i]
    target = [entry / square for entry in normal]

    def back(right):
        right, solved = list(right), [None] * COLS
        for j in range(COLS - 1, -1, -1):
            solved[j] = right[j] * inverse[j]
            for i in range(j):
                right[i] = right[i] - factor[(i, j)] * solved[j]
        return solved

    z = back(target)
    z_parts = [split(entry) for entry in z]
    missing = []
    for i in range(COLS):
        high, low = target[i], None
        for j in range(i, COLS):
            (ah, al), (bh, bl) = split(factor[(i, j)]), z_parts[j]
            product = factor[(i, j)] * z[j]
            error = ((ah * bh - product) + ah * bl + al * bh) + al * bl
            high, carry = two_sum(high, -product)
            carry = carry - error
            low = carry if low is None else low + carry
        missing.append(high + low)
    z = [a + b for a, b in zip(z, back(missing))]

    y = [None] * STEPS
    for j in range(STEPS, 0, -1):
        right = -z[j]
        if j < STEPS:
            right = right - shifts[j] * y[j]
        y[j - 1] = right * (1.0 / spread_scale)
    return y, 1.0 / jnp.sqrt(square), z


def combine_kernel(basis, rows, correction, remainder, upper, norm):
    stacked = rows[...].T
    tops = [stacked[8 * j : 8 * j + 8] for j in range(COLS)]
    tail = stacked[8 * COLS : 8 * COLS + 8]
    sublane = lax.broadcasted_iota(jnp.int32, (8, 128), 0)
    tail = jnp.where(sublane == 0, tail, 0.0)
    factor = {}
    for k in range(COLS):
        square = tops[k] * tops[k]
        if k == COLS - 1:
            square = square + tail * tail
        dots = [total(square)] + [total(tops[k] * tops[j]) for j in range(k + 1, COLS)]
        ridge = dots[0] + 1e-12
        length = jnp.sqrt(ridge)
        again = 2.0 - dots[0] / ridge
        factor[(k, k)] = length
        for j in range(k + 1, COLS):
            factor[(k, j)] = dots[j - k] / length * again
            tops[j] = tops[j] - (dots[j - k] / ridge * again) * tops[k]

    y, size, z = small_solve(factor)

    line = lax.broadcasted_iota(jnp.int32, (16, 128), 0)
    lane = lax.broadcasted_iota(jnp.int32, (16, 128), 1)
    table = jnp.zeros((16, 128), jnp.float32)
    for (i, j), entry in factor.items():
        table = jnp.where(jnp.logical_and(line == i, lane == j), entry, table)
    upper[...] = table[:COLS, :COLS]
    norm[...] = size

    size_x, size_y, _ = correction.shape
    long_y = size_y + 2 * HALO

    def combine(x, _):
        rows = pl.ds(pl.multiple_of((x + HALO) * long_y + HALO, 8), size_y)
        here = basis[0, rows, :]
        first, second = y[0] * here, z[0] * here
        for j in range(1, COLS):
            here = basis[j, rows, :]
            if j < STEPS:
                first = first + y[j] * here
            second = second + z[j] * here
        correction[x] = first
        remainder[x] = second
        return 0

    lax.fori_loop(0, size_x, combine, 0, unroll=4)


def combine(shape, basis, rows):
    block = jax.ShapeDtypeStruct(shape, jnp.float32)
    return pl.pallas_call(
        combine_kernel,
        out_shape=(
            block,
            block,
            jax.ShapeDtypeStruct((COLS, COLS), jnp.float32),
            jax.ShapeDtypeStruct((1, 1), jnp.float32),
        ),
        in_specs=vmem_spec(2),
        out_specs=tuple(vmem_spec(4)),
        compiler_params=pltpu.CompilerParams(vmem_limit_bytes=8 * MIB),
        name="combine",
    )(basis, rows)


def on_device(source, conduct, storage):
    inner, outer, near, far = edges(source, conduct, storage)
    rows = exchange(inner, outer, "narrow")
    beyond = swap(far, "wide", 1)
    near_all, far_tiles = corners(*rows, near, beyond)
    tiles = exchange(near_all, far_tiles, "wide")
    basis, packed = basis_and_factor(near, far, *rows, tiles[0], beyond, tiles[1])
    gathered = lax.all_to_all(packed, ("wide", "narrow"), 0, 0, tiled=True)
    correction, remainder, factor, resid = combine(source.shape, basis, gathered)
    return correction, remainder, factor, resid[0, 0]


def solution(mesh):
    spec = P("wide", "narrow", None)
    return jax.shard_map(
        on_device,
        mesh=mesh,
        in_specs=(spec, spec, spec),
        out_specs=(spec, spec, P(), P()),
        check_vma=False,
    )
```

```python
import math

import jax
import jax.numpy as jnp
from jax import lax
from jax.experimental import pallas as pl
from jax.experimental.pallas import tpu as pltpu
from jax.sharding import PartitionSpec as P

STEPS = 8
COLS = 9
HALO = 8

leja_order = (0, 7, 3, 5, 2, 6, 1, 4)
spread_scale = 6.5
MIB = 1024 * 1024


def newton_shifts():
    return [
        13.125 + 12.875 * math.cos(math.pi * (2 * position + 1) / 16.0) for position in leja_order
    ]


def is_odd(axis):
    return lax.rem(lax.axis_index(axis), 2) == 1


def swap(block, axis, shift):
    axes = ("wide", "narrow")
    sizes = [lax.axis_size(name) for name in axes]
    along = axes.index(axis)
    pairs = []
    for i in range(sizes[0]):
        for j in range(sizes[1]):
            to = [i, j]
            to[along] = (to[along] + shift ^ 1) - shift
            if not 0 <= to[along] < sizes[along]:
                to = [i, j]
                to[1 - along] ^= 1
            pairs.append((i * sizes[1] + j, to[0] * sizes[1] + to[1]))
    return lax.ppermute(block, axes, pairs)


def exchange(inner, outer, axis):
    return swap(inner, axis, 0), swap(outer, axis, 1)


def vmem_spec(count):
    return [pl.BlockSpec(memory_space=pltpu.VMEM)] * count


def edge_kernel(source, conduct, storage, inner, outer, near, far, sems):
    odd_n, odd_w = is_odd("narrow"), is_odd("wide")
    size_x, width, _ = source.shape
    half = size_x // 2

    for flag_n in (False, True):
        for flag_w in (False, True):

            @pl.when(jnp.logical_and(odd_n == flag_n, odd_w == flag_w))
            def _(flag_n=flag_n, flag_w=flag_w):
                low, high = (inner, outer) if flag_n else (outer, inner)
                halves = (near, far) if flag_w else (far, near)
                copies = []
                for k, ref in enumerate((source, conduct, storage)):
                    for side, out in enumerate(halves):
                        block = ref.at[pl.ds(side * half, half)]
                        copies.append(
                            pltpu.make_async_copy(block, out.at[k], sems.at[2 * k + side])
                        )
                for copy in copies:
                    copy.start()
                for copy in copies:
                    copy.wait()
                for side, out in enumerate(halves):
                    planes = pl.ds(side * half, half)
                    low[:, planes] = out[:, :, 0:HALO, :]
                    high[:, planes] = out[:, :, width - HALO : width, :]


def edges(source, conduct, storage):
    size_x, width, size_z = source.shape
    rows = jax.ShapeDtypeStruct((3, size_x, HALO, size_z), jnp.float32)
    halves = jax.ShapeDtypeStruct((3, size_x // 2, width, size_z), jnp.float32)
    return pl.pallas_call(
        edge_kernel,
        out_shape=(rows, rows, halves, halves),
        in_specs=[pl.BlockSpec(memory_space=pltpu.HBM)] * 3,
        out_specs=tuple(vmem_spec(4)),
        scratch_shapes=[pltpu.SemaphoreType.DMA((6,))],
        compiler_params=pltpu.CompilerParams(vmem_limit_bytes=8 * MIB),
        name="edges",
    )(*(pltpu.with_memory_space_constraint(x, pltpu.HBM) for x in (source, conduct, storage)))


def corner_kernel(inner, outer, own, _, near, far):
    odd_n, odd_w = is_odd("narrow"), is_odd("wide")
    half = near.shape[1]
    row = lax.broadcasted_iota(jnp.int32, far.shape[2:], 0)
    for k in range(3):
        for p in range(half):
            near[k, p, HALO:, :] = own[k, p]

    def fill(low_rows, high_rows, low_half, high_half):
        for k in range(3):
            for p in range(half):
                low_half[k, p, 0:HALO, :] = jnp.where(
                    row >= p + 1, low_rows[k, p], high_rows[k, half - 1 - p]
                )
                high_half[k, p, 0:HALO, :] = jnp.where(
                    row >= half - p, low_rows[k, half + p], high_rows[k, 2 * half - 1 - p]
                )

    for flag_n in (False, True):
        for flag_w in (False, True):

            @pl.when(jnp.logical_and(odd_n == flag_n, odd_w == flag_w))
            def _(flag_n=flag_n, flag_w=flag_w):
                rows = (inner, outer) if flag_n else (outer, inner)
                halves = (near, far) if flag_w else (far, near)
                fill(*rows, *halves)


def corners(inner, outer, own, wait):
    _, size_x, rows, size_z = inner.shape
    shape = lambda count: jax.ShapeDtypeStruct((3, size_x // 2, count, size_z), jnp.float32)
    return pl.pallas_call(
        corner_kernel,
        out_shape=(shape(rows + own.shape[2]), shape(rows)),
        in_specs=vmem_spec(4),
        out_specs=tuple(vmem_spec(2)),
        compiler_params=pltpu.CompilerParams(vmem_limit_bytes=8 * MIB),
        name="corners",
    )(inner, outer, own, wait)


def total(x):
    return jnp.sum(jnp.sum(x, axis=0, keepdims=True), axis=1, keepdims=True)


def basis_kernel(
    last, long_y, near, far, rows_inner, rows_outer, planes_inner, planes_outer,
    corner_outer, basis, rows_out,
    cond, diag, face_x, face_y, face_yp, face_z, face_zp,
    back_a, front_a, back_b, front_b, work,
):
    odd_w = is_odd("wide")
    place_w, place_n = lax.axis_index("wide"), lax.axis_index("narrow")
    keep_left = jnp.where(place_w == 0, 0.0, 1.0)
    keep_right = jnp.where(place_w == last[0], 0.0, 1.0)
    keep_low = jnp.where(place_n == 0, 0.0, 1.0)
    keep_high = jnp.where(place_n == last[1], 0.0, 1.0)
    field = basis.at[0]
    size_z = diag.shape[1]
    long_x = diag.shape[0] // long_y
    size_x, size_y = long_x - 2 * HALO, long_y - 2 * HALO
    shifts = newton_shifts()

    def at(x, count=long_y, first=0):
        start = x * long_y + first
        if not isinstance(x, int) and first % 8 == 0:
            start = pl.multiple_of(start, 8)
        return pl.ds(start, count)

    targets = ((field, 0), (cond, long_y), (diag, 0))

    def place_own(low, high, first, second):
        half = size_x // 2
        for k, (out, skip) in enumerate(targets):
            for p in range(size_x):
                start = skip + (HALO + p) * long_y
                out[pl.ds(start, HALO), :] = low[k, p] * keep_low
                own = first[k, p] if p < half else second[k, p - half]
                out[pl.ds(start + HALO, size_y), :] = own
                out[pl.ds(start + HALO + size_y, HALO), :] = high[k, p] * keep_high

    def place_beside(first, planes, tiles, keep):
        for k, (out, skip) in enumerate(targets):
            for p in range(HALO):
                start = skip + (first + p) * long_y
                own = planes[k, p, planes.shape[2] - size_y :, :]
                out[pl.ds(start, HALO), :] = tiles[k, p, 0:HALO, :] * (keep * keep_low)
                out[pl.ds(start + HALO, size_y), :] = own * keep
                out[pl.ds(start + HALO + size_y, HALO), :] = tiles[
                    k, HALO - 1 - p, 0:HALO, :
                ] * (keep * keep_high)

    odd_n = is_odd("narrow")
    for flag_n in (False, True):
        for flag_w in (False, True):

            @pl.when(jnp.logical_and(odd_n == flag_n, odd_w == flag_w))
            def _(flag_n=flag_n, flag_w=flag_w):
                rows = (rows_inner, rows_outer) if flag_n else (rows_outer, rows_inner)
                place_own(*rows, *((near, far) if flag_w else (far, near)))

    @pl.when(odd_w)
    def _():
        place_beside(0, planes_inner, planes_inner, keep_left)
        place_beside(HALO + size_x, planes_outer, corner_outer, keep_right)

    @pl.when(jnp.logical_not(odd_w))
    def _():
        place_beside(0, planes_outer, corner_outer, keep_left)
        place_beside(HALO + size_x, planes_inner, planes_inner, keep_right)

    empty = jnp.zeros((long_y, size_z), jnp.float32)
    cond[at(0), :] = empty
    cond[at(long_x + 1), :] = empty

    lane = lax.broadcasted_iota(jnp.int32, (long_y, size_z), 1)
    row = lax.broadcasted_iota(jnp.int32, (long_y, size_z), 0)
    unit = 1.0 / spread_scale
    half = 0.5 * unit
    mask_y = jnp.where(row == HALO, keep_low, jnp.where(row == HALO + size_y, keep_high, 1.0))
    mask_yp = jnp.where(
        row == HALO - 1, keep_low, jnp.where(row == HALO + size_y - 1, keep_high, 1.0)
    )

    def turn(value):
        return (
            jnp.where(lane == 0, 0.0, pltpu.roll(value, 1, 1)),
            jnp.where(lane == size_z - 1, 0.0, pltpu.roll(value, size_z - 1, 1)),
        )

    def turn_start(x):
        here = field[at(x), :]
        back_a[at(x), :] = pltpu.roll(here, 1, 1)
        front_a[at(x), :] = pltpu.roll(here, size_z - 1, 1)
        back, front = turn(cond[at(x + 1), :])
        back_b[at(x), :] = back
        front_b[at(x), :] = front

    def coefficients(x):
        here = cond[at(x + 1), :]
        left = half * (here + cond[at(x), :])
        right = half * (here + cond[at(x + 2), :])
        low = half * (here + cond[at(x + 1, long_y, -1), :])
        high = half * (here + cond[at(x + 1, long_y, 1), :])
        z_low = half * (here + back_b[at(x), :])
        z_high = half * (here + front_b[at(x), :])
        face_x[at(x), :] = left
        face_y[at(x), :] = low * mask_y
        face_yp[at(x), :] = high * mask_yp
        face_z[at(x), :] = jnp.where(lane == 0, 0.0, z_low)
        face_zp[at(x), :] = jnp.where(lane == size_z - 1, 0.0, z_high)
        diag[at(x), :] = unit * diag[at(x), :] + ((left + right) + (low + high) + (z_low + z_high))

    group = 16

    def start_group(g, _):
        for i in range(group):
            coefficients((g - 1) * group + i)
        for i in range(group):
            turn_start(g * group + i)
        return 0

    for i in range(group):
        turn_start(i)
    lax.fori_loop(1, long_x // group, start_group, 0)
    for i in range(group):
        coefficients(long_x - group + i)
    face_x[at(HALO), :] = face_x[at(HALO), :] * keep_left
    face_x[at(HALO + size_x), :] = face_x[at(HALO + size_x), :] * keep_right

    group = 12

    def step(number, read, back, front, write, next_back, next_front):
        theta = shifts[number] * unit
        final = number == STEPS - 1
        low, count = (HALO, size_y) if final else (0, long_y)

        def plane(x):
            rows = at(x, count, low)
            here = read[rows, :]
            beside = (
                face_x[at(x + 1, count, low), :] * read[at(x + 1, count, low), :]
                + face_x[rows, :] * read[at(x - 1, count, low), :]
            )
            across = (
                face_yp[rows, :] * read[at(x, count, low + 1), :]
                + face_y[rows, :] * read[at(x, count, low - 1), :]
            )
            along = face_zp[rows, :] * front[rows, :] + face_z[rows, :] * back[rows, :]
            write[rows, :] = (diag[rows, :] - theta) * here - (beside + across + along)

        def turn_plane(x):
            if not final:
                rows = at(x, size_y, HALO) if number == STEPS - 2 else at(x)
                here = write[rows, :]
                next_back[rows, :] = pltpu.roll(here, 1, 1)
                next_front[rows, :] = pltpu.roll(here, size_z - 1, 1)

        start, stop = number + 1, long_x - 1 - number
        head = (stop - start) % group or group
        for x in range(start, start + head):
            plane(x)
        for x in range(start + 1, start + head):
            turn_plane(x)
        begin = start + head
        for x in range(begin, begin + group):
            plane(x)

        def body(g, _):
            x = begin + g * group
            for i in range(group):
                turn_plane(x - group + i)
            for i in range(group):
                plane(x + i)
            return 0

        lax.fori_loop(1, (stop - begin) // group, body, 0)
        for x in range(stop - group, stop - 1):
            turn_plane(x)

    turned = ((back_a, front_a), (back_b, front_b))
    for number in range(STEPS):
        step(
            number, basis.at[number], *turned[number % 2],
            basis.at[number + 1], *turned[(number + 1) % 2],
        )

    def own(x):
        return at(x + HALO, size_y, HALO)

    def fold(product):
        parts = [product[8 * t : 8 * t + 8] for t in range(size_y // 8)]
        while len(parts) > 1:
            parts = [a + b for a, b in zip(parts[::2], parts[1::2])]
        return parts[0]

    zero = jnp.zeros((8, size_z), jnp.float32)

    def first_dots(x, sums):
        columns = [basis[j, own(x), :] for j in range(COLS)]
        return tuple(s + fold(columns[0] * c) for s, c in zip(sums, columns))

    sums = lax.fori_loop(0, size_x, first_dots, (zero,) * COLS, unroll=True)
    dots = [total(s) for s in sums]
    index = lax.broadcasted_iota(jnp.int32, (1, 128), 1)
    packed = jnp.zeros((1, 128), jnp.float32)
    for k in range(COLS):
        length = jnp.sqrt(dots[0])
        inverse = jnp.where(dots[0] > 0.0, 1.0 / length, 0.0)
        ratio = [d * inverse * inverse for d in dots]
        for j in range(k, COLS):
            entry = length if j == k else dots[j - k] * inverse
            packed = jnp.where(index == 8 * j + k, entry, packed)
        if k == COLS - 1:
            break

        def sweep(x, sums, k=k, ratio=ratio):
            pivot = field[own(x), :] if k == 0 else work[k, x]
            columns = []
            for j in range(k + 1, COLS):
                old = basis[j, own(x), :] if k == 0 else work[j, x]
                new = old - ratio[j - k] * pivot
                work[j, x] = new
                columns.append(new)
            return tuple(s + fold(columns[0] * c) for s, c in zip(sums, columns))

        sums = lax.fori_loop(
            0, size_x, sweep, (zero,) * (COLS - 1 - k), unroll=True
        )
        dots = [total(s) for s in sums]
    rows_out[...] = jnp.broadcast_to(packed, rows_out.shape)


def basis_and_factor(*parts):
    _, half, size_y, size_z = parts[0].shape
    size_x = 2 * half
    long_x, long_y = size_x + 2 * HALO, size_y + 2 * HALO
    devices = lax.axis_size("wide") * lax.axis_size("narrow")
    last = (lax.axis_size("wide") - 1, lax.axis_size("narrow") - 1)
    planes = lambda count: pltpu.VMEM((count * long_y, size_z), jnp.float32)
    return pl.pallas_call(
        lambda *refs: basis_kernel(last, long_y, *refs),
        out_shape=(
            jax.ShapeDtypeStruct((COLS, long_x * long_y, size_z), jnp.float32),
            jax.ShapeDtypeStruct((devices, 128), jnp.float32),
        ),
        in_specs=vmem_spec(7),
        out_specs=tuple(vmem_spec(2)),
        scratch_shapes=[planes(long_x + 2)] + [planes(long_x)] * 10
        + [pltpu.VMEM((COLS, size_x, size_y, size_z), jnp.float32)],
        compiler_params=pltpu.CompilerParams(vmem_limit_bytes=28 * MIB),
        name="basis_and_factor",
    )(*parts)


def split(x):
    big = x * 4097.0
    high = big - (big - x)
    return high, x - high


def two_sum(a, b):
    s = a + b
    t = s - a
    return s, (a - (s - t)) + (b - t)


def small_solve(factor):
    shifts = newton_shifts()
    null = [1.0]
    for theta in shifts:
        null.append(-theta / spread_scale * null[-1])
    inverse = [1.0 / factor[(i, i)] for i in range(COLS)]

    left = [jnp.full((1, 1), w, jnp.float32) for w in null]
    normal = []
    for i in range(COLS):
        normal.append(left[i] * inverse[i])
        for j in range(i + 1, COLS):
            left[j] = left[j] - factor[(i, j)] * normal[i]
    square = normal[0] * normal[0]
    for i in range(1, COLS):
        square = square + normal[i] * normal[i]
    target = [entry / square for entry in normal]

    def back(right):
        right, solved = list(right), [None] * COLS
        for j in range(COLS - 1, -1, -1):
            solved[j] = right[j] * inverse[j]
            for i in range(j):
                right[i] = right[i] - factor[(i, j)] * solved[j]
        return solved

    z = back(target)
    z_parts = [split(entry) for entry in z]
    missing = []
    for i in range(COLS):
        high, low = target[i], None
        for j in range(i, COLS):
            (ah, al), (bh, bl) = split(factor[(i, j)]), z_parts[j]
            product = factor[(i, j)] * z[j]
            error = ((ah * bh - product) + ah * bl + al * bh) + al * bl
            high, carry = two_sum(high, -product)
            carry = carry - error
            low = carry if low is None else low + carry
        missing.append(high + low)
    z = [a + b for a, b in zip(z, back(missing))]

    y = [None] * STEPS
    for j in range(STEPS, 0, -1):
        right = -z[j]
        if j < STEPS:
            right = right - shifts[j] * y[j]
        y[j - 1] = right * (1.0 / spread_scale)
    return y, 1.0 / jnp.sqrt(square), z


def combine_kernel(basis, rows, correction, remainder, upper, norm):
    stacked = rows[...].T
    tops = [stacked[8 * j : 8 * j + 8] for j in range(COLS)]
    tail = stacked[8 * COLS : 8 * COLS + 8]
    sublane = lax.broadcasted_iota(jnp.int32, (8, 128), 0)
    tail = jnp.where(sublane == 0, tail, 0.0)
    factor = {}
    for k in range(COLS):
        square = tops[k] * tops[k]
        if k == COLS - 1:
            square = square + tail * tail
        dots = [total(square)] + [total(tops[k] * tops[j]) for j in range(k + 1, COLS)]
        ridge = dots[0] + 1e-12
        inverse = 1.0 / ridge
        again = 2.0 - dots[0] * inverse
        scale = inverse * again
        length = jnp.sqrt(ridge)
        factor[(k, k)] = length
        for j in range(k + 1, COLS):
            tops[j] = tops[j] - (dots[j - k] * scale) * tops[k]
            factor[(k, j)] = dots[j - k] * (length * scale)

    y, size, z = small_solve(factor)

    line = lax.broadcasted_iota(jnp.int32, (16, 128), 0)
    lane = lax.broadcasted_iota(jnp.int32, (16, 128), 1)
    table = jnp.zeros((16, 128), jnp.float32)
    for (i, j), entry in factor.items():
        table = jnp.where(jnp.logical_and(line == i, lane == j), entry, table)
    upper[...] = table[:COLS, :COLS]
    norm[...] = size

    size_x, size_y, _ = correction.shape
    long_y = size_y + 2 * HALO

    def combine(x, _):
        rows = pl.ds(pl.multiple_of((x + HALO) * long_y + HALO, 8), size_y)
        here = basis[0, rows, :]
        first, second = y[0] * here, z[0] * here
        for j in range(1, COLS):
            here = basis[j, rows, :]
            if j < STEPS:
                first = first + y[j] * here
            second = second + z[j] * here
        correction[x] = first
        remainder[x] = second
        return 0

    lax.fori_loop(0, size_x, combine, 0, unroll=4)


def combine(shape, basis, rows):
    block = jax.ShapeDtypeStruct(shape, jnp.float32)
    return pl.pallas_call(
        combine_kernel,
        out_shape=(
            block,
            block,
            jax.ShapeDtypeStruct((COLS, COLS), jnp.float32),
            jax.ShapeDtypeStruct((1, 1), jnp.float32),
        ),
        in_specs=vmem_spec(2),
        out_specs=tuple(vmem_spec(4)),
        compiler_params=pltpu.CompilerParams(vmem_limit_bytes=8 * MIB),
        name="combine",
    )(basis, rows)


def on_device(source, conduct, storage):
    inner, outer, near, far = edges(source, conduct, storage)
    rows = exchange(inner, outer, "narrow")
    beyond = swap(far, "wide", 1)
    near_all, far_tiles = corners(*rows, near, beyond)
    tiles = exchange(near_all, far_tiles, "wide")
    basis, packed = basis_and_factor(near, far, *rows, tiles[0], beyond, tiles[1])
    gathered = lax.all_to_all(packed, ("wide", "narrow"), 0, 0, tiled=True)
    correction, remainder, factor, resid = combine(source.shape, basis, gathered)
    return correction, remainder, factor, resid[0, 0]


def solution(mesh):
    spec = P("wide", "narrow", None)
    return jax.shard_map(
        on_device,
        mesh=mesh,
        in_specs=(spec, spec, spec),
        out_specs=(spec, spec, P(), P()),
        check_vma=False,
    )
```
